512 devices in a mesh: xy: 32 (over y, x), gz: 16 (over z, core).
Axes of the slice: x: 4, y: 8, z: 8, core: 2. Of those that a mesh axis runs over, the one named last changes fastest.
Arguments:
- volume: float32 [1536, 32768], P('gz', 'xy'), may hold values from 0 to 1
- sinogram: float32 [1536, 8192], P('gz', 'xy'), may hold values from 100 to 2000
- ray_mats: bfloat16 [32, 16, 256, 256], P('xy'), may hold values from 0.049804688 to 1
- offsets: int32 [32, 16], P('xy'), may hold values from 0 to 768
- ray_lists: int32 [32, 16], replicated, may hold values from 0 to 31, all different within a row
- owner_map: int32 [32], replicated, may hold values from 0 to 31, each once
Outputs:
- new_volume: float32 [1536, 32768], P('gz', 'xy')
- weighted: float32 [1536, 8192], P('gz', 'xy')
The draws below stay inside these ranges and needn't reach their ends.
Inputs may be any that keep to these rules, and one draw needn't show every extreme that they name: `ray_lists`: the 16 entries of a row are distinct, and every ray block is named by some row. `owner_map`: each owner appears once.
All inputs are finite; a program needn't handle non-finite values.
Results may differ from the reference program's by a relative error of at most 0.0003.
Values sent between devices are 32-bit elements; how exact they have to be, the bound alone decides.
No kernel may reach another device: no remote copies, remote signals or barrier semaphores. Data moves between devices by JAX's collectives and lax.ppermute only.
A program may use at most 64 MiB of HBM per device.

```python
import jax
import jax.numpy as jnp
from jax import lax

VXY = 1024
W = 256
RB = 256
K = 16
NZ = 1536
VOX = 32768
BLOCKS = 32


def set_ends(drawn, rng, low, top_value):
    index_at = [jax.random.randint(jax.random.fold_in(rng, axis), (), 0, length) for axis, length in enumerate(drawn.shape)]
    widest = drawn.shape.index(max(drawn.shape))
    next_to = index_at[:widest] + [(index_at[widest] + 1) % drawn.shape[widest]] + index_at[widest + 1:]
    return drawn.at[tuple(index_at)].set(low).at[tuple(next_to)].set(top_value)


def block_scale(rng, extent, pieces, smallest, top_value):
    gain = 1.0
    for dim, shards_of in pieces:
        steps = jax.random.uniform(jax.random.fold_in(jax.random.fold_in(rng, 6), dim), (shards_of,), jnp.float32, smallest / len(pieces), top_value / len(pieces))
        gain = gain * jnp.repeat(jnp.exp(steps), extent[dim] // shards_of).reshape((-1,) + (1,) * (len(extent) - 1 - dim))
    return gain


def different_ones(key, rows, count, top, lift):
    sequence = jax.random.permutation(jax.random.fold_in(key, 1), count)
    pull = sequence
    for power in range(3):
        pull = pull * pull // count
    pull = pull * lift // count
    tickets = jax.random.randint(jax.random.fold_in(key, 2), (rows, count), 0, 4096) + pull
    sure = jax.random.permutation(jax.random.fold_in(key, 3), rows)[jnp.arange(count) % rows]
    tickets = jnp.where(jnp.arange(rows)[:, None] == sure[None, :], 1 << 14, tickets)
    merit = tickets * count + jnp.arange(count)
    return lax.top_k(merit.astype(jnp.int32), top)[1].astype(jnp.int32)


def setup_inputs(seed: int = 0) -> dict:
    key_list = jax.random.split(jax.random.key(seed), 7)
    volume = jnp.clip(1.0 * jax.random.uniform(key_list[0], (NZ, VOX), jnp.float32) ** block_scale(key_list[0], (NZ, VOX), ((0, 16), (1, 32)), -0.2, 0.2), 0.0, 1.0)
    sinogram = jnp.clip(100.0 + 1900.0 * jax.random.uniform(key_list[1], (NZ, BLOCKS * RB), jnp.float32) ** block_scale(key_list[1], (NZ, BLOCKS * RB), ((0, 16), (1, 32)), -0.2, 0.2), 100.0, 2000.0)
    ray_mats = jnp.clip(0.049804688 + 0.9501953 * jax.random.uniform(key_list[2], (BLOCKS, K, W, RB), jnp.float32) ** block_scale(key_list[2], (BLOCKS, K, W, RB), ((0, 32),), -0.2, 0.2), 0.049804688, 1.0).astype(jnp.bfloat16)
    offsets = set_ends(jax.random.randint(key_list[3], (BLOCKS, K), 0, VXY - W + 1), jax.random.fold_in(key_list[3], 1), 0, VXY - W).astype(jnp.int32)
    ray_lists = different_ones(key_list[4], BLOCKS, BLOCKS, K, 4096)
    owner_map = jax.random.permutation(key_list[5], BLOCKS).astype(jnp.int32)
    return dict(volume=volume, sinogram=sinogram, ray_mats=ray_mats, offsets=offsets, ray_lists=ray_lists, owner_map=owner_map)


relax = 1.0
tv_weight = 0.2
smooth_sq = 0.01

def cut_windows(field, starts, width):
    return jax.vmap(lambda start: lax.dynamic_slice_in_dim(field, start, width, 1))(starts)

def spread_back(smeared, column_terms, starts, vxy):
    depth = smeared.shape[1]
    width = smeared.shape[2]

    def add_one(index, carry):
        update, column = carry
        start = starts[index]
        piece = lax.dynamic_slice_in_dim(update, start, width, 1) + smeared[index]
        update = lax.dynamic_update_slice_in_dim(update, piece, start, 1)
        col_piece = lax.dynamic_slice_in_dim(column, start, width, 0) + column_terms[index]
        column = lax.dynamic_update_slice_in_dim(column, col_piece, start, 0)
        return (update, column)
    init = (jnp.zeros((depth, vxy), jnp.float32), jnp.zeros((vxy,), jnp.float32))
    return lax.fori_loop(0, smeared.shape[0], add_one, init)

def total_variation(padded):
    diffs = padded[1:] - padded[:-1]
    slopes = diffs / jnp.sqrt(diffs * diffs + smooth_sq)
    return slopes[:-1] - slopes[1:]

def reference(volume, sinogram, ray_mats, offsets, ray_lists, owner_map):
    nblk = ray_mats.shape[0]
    width = ray_mats.shape[2]
    rays = ray_mats.shape[3]
    depth = volume.shape[0]
    vxy = volume.shape[1] // nblk
    blocks = volume.reshape(depth, nblk, vxy).transpose(1, 0, 2)
    owners = owner_map[ray_lists]
    order = jnp.arange(nblk, dtype=jnp.int32)

    def project(carry, block_index):
        proj, rowsum = carry
        block = blocks[block_index]
        matrix = ray_mats[block_index].astype(jnp.float32)
        windows = cut_windows(block, offsets[block_index], width)
        partial_value = jnp.einsum('kzw,kwr->kzr', windows, matrix, precision=lax.Precision.HIGHEST)
        proj = proj.at[owners[block_index]].add(partial_value)
        rowsum = rowsum.at[owners[block_index]].add(lax.optimization_barrier(jnp.sum(matrix, axis=1)))
        return ((proj, rowsum), None)
    init = (jnp.zeros((nblk, depth, rays), jnp.float32), jnp.zeros((nblk, rays), jnp.float32))
    (proj, rowsum), _ = lax.scan(project, init, order)
    measured = sinogram.reshape(depth, nblk, rays).transpose(1, 0, 2)
    weighted = (measured - proj) / rowsum[:, None, :]

    def backproject(block_index):
        matrix = ray_mats[block_index].astype(jnp.float32)
        needed = weighted[owners[block_index]]
        smeared = jnp.einsum('kzr,kwr->kzw', needed, matrix, precision=lax.Precision.HIGHEST)
        update, column = spread_back(smeared, lax.optimization_barrier(jnp.sum(matrix, axis=2)), offsets[block_index], vxy)
        return update / jnp.maximum(column, 1.0)[None, :]
    updates = lax.map(backproject, order)
    update = updates.transpose(1, 0, 2).reshape(depth, nblk * vxy)
    padded = jnp.pad(volume, ((1, 1), (0, 0)))
    new_volume = volume + relax * update - tv_weight * total_variation(padded)
    weighted_out = weighted.transpose(1, 0, 2).reshape(depth, nblk * rays)
    return (new_volume, weighted_out)
```

```python
import jax
import jax.numpy as jnp
from jax import lax
from jax.experimental import pallas as pl
from jax.experimental.pallas import tpu as pltpu
from jax.sharding import PartitionSpec as P

relax = 1.0
tv_weight = 0.2
smooth_sq = 0.01

NX, NY = 4, 8
PAIRS = NY // 2
W = 256
LANES = 128
VMEM_LIMIT = 40 * 1024 * 1024


def device_of(pair, odd, x):
    return (2 * pair + odd) * NX + x


NEAR = [[device_of(p, q, x) for q in range(2) for x in range(NX)] for p in range(PAIRS)]
FAR = [[device_of(p, q, x) for p in range(PAIRS)] for q in range(2) for x in range(NX)]


def exchange(value, groups):
    return lax.all_to_all(
        value, "xy", split_axis=0, concat_axis=0, axis_index_groups=groups, tiled=True
    )


def split3(value):
    high = value.astype(jnp.bfloat16)
    rest = value - high.astype(jnp.float32)
    mid = rest.astype(jnp.bfloat16)
    low = (rest - mid.astype(jnp.float32)).astype(jnp.bfloat16)
    return [high, mid, low]


def with_ones(value):
    ones = jnp.ones((16, value.shape[1]), jnp.bfloat16)
    return jnp.concatenate(split3(value) + [ones], axis=0)


def near_far(owner):
    y, x = owner // NX, owner % NX
    return (y % 2) * NX + x, y // 2


def project_kernel(me_ref, lists_ref, owners_ref, starts_ref, vol_ref, mats_ref, out_ref, wide):
    rows = vol_ref.shape[0]
    count = starts_ref.shape[1]
    wide[:, : vol_ref.shape[1]] = vol_ref[...]
    wide[:, vol_ref.shape[1] :] = jnp.zeros((rows, LANES), jnp.float32)
    out_ref[...] = jnp.zeros(out_ref.shape, jnp.float32)
    me = me_ref[0]

    def step(k, carry):
        start = starts_ref[0, k]
        near, far = near_far(owners_ref[lists_ref[me, k]])
        base = pl.multiple_of((start // LANES) * LANES, LANES)
        window = wide[:, pl.ds(base, W + LANES)]
        window = pltpu.roll(window, (W + LANES) - start % LANES, 1)[:, :W]
        product = jnp.dot(
            with_ones(window), mats_ref[0, k], preferred_element_type=jnp.float32
        )
        value = product[2 * rows : 3 * rows] + product[rows : 2 * rows] + product[:rows]
        out_ref[near, pl.ds(pl.multiple_of(far * rows, 8), rows), :] = value
        out_ref[near, pl.ds(PAIRS * rows + far, 1), :] = product[3 * rows : 3 * rows + 1]
        return carry

    lax.fori_loop(0, count, step, 0, unroll=2)


def project(me, lists, owners, starts, volume, mats):
    rows, cols = volume.shape
    smem = pl.BlockSpec(memory_space=pltpu.SMEM)
    vmem = pl.BlockSpec(memory_space=pltpu.VMEM)
    return pl.pallas_call(
        project_kernel,
        out_shape=jax.ShapeDtypeStruct((2 * NX, PAIRS * rows + 8, W), jnp.float32),
        in_specs=[smem] * 4 + [vmem] * 2,
        out_specs=vmem,
        scratch_shapes=[pltpu.VMEM((rows, cols + LANES), jnp.float32)],
        compiler_params=pltpu.CompilerParams(vmem_limit_bytes=VMEM_LIMIT),
    )(me, lists, owners, starts, volume, mats)


def back_kernel(
    me_ref, lists_ref, owners_ref, starts_ref, base_ref, mats_ref, got_ref, out_ref, total
):
    rows, cols = base_ref.shape
    count = starts_ref.shape[1]
    total[...] = jnp.zeros(total.shape, jnp.float32)
    me = me_ref[0]

    def step(k, carry):
        start = starts_ref[0, k]
        near, far = near_far(owners_ref[lists_ref[me, k]])
        base = pl.multiple_of((start // LANES) * LANES, LANES)
        product = lax.dot_general(
            with_ones(got_ref[near, far]),
            mats_ref[0, k],
            (((1,), (1,)), ((), ())),
            preferred_element_type=jnp.float32,
        )
        value = product[2 * rows : 3 * rows] + product[rows : 2 * rows] + product[:rows]
        value = jnp.concatenate([value, product[3 * rows : 3 * rows + 8]], axis=0)
        value = jnp.concatenate([value, jnp.zeros((rows + 8, LANES), jnp.float32)], axis=1)
        total[:, pl.ds(base, W + LANES)] += pltpu.roll(value, start % LANES, 1)
        return carry

    lax.fori_loop(0, count, step, 0, unroll=2)
    column = jnp.maximum(total[rows : rows + 1, :cols], 1.0)
    out_ref[...] = base_ref[...] + relax * (total[:rows, :cols] / column)


def back_project(me, lists, owners, starts, base, mats, got):
    rows, cols = base.shape
    smem = pl.BlockSpec(memory_space=pltpu.SMEM)
    vmem = pl.BlockSpec(memory_space=pltpu.VMEM)
    return pl.pallas_call(
        back_kernel,
        out_shape=jax.ShapeDtypeStruct((rows, cols), jnp.float32),
        in_specs=[smem] * 4 + [vmem] * 3,
        out_specs=vmem,
        scratch_shapes=[pltpu.VMEM((rows + 8, cols + LANES), jnp.float32)],
        compiler_params=pltpu.CompilerParams(vmem_limit_bytes=VMEM_LIMIT),
    )(me, lists, owners, starts, base, mats, got)


def with_faces(volume):
    count = lax.axis_size("gz")
    up = [(i, i + 1) for i in range(count - 1)]
    down = [(i + 1, i) for i in range(count - 1)]
    return jnp.concatenate(
        [
            lax.ppermute(volume[-1:], "gz", up),
            volume,
            lax.ppermute(volume[:1], "gz", down),
        ],
        axis=0,
    )


def total_variation(padded):
    diffs = padded[1:] - padded[:-1]
    slopes = diffs / jnp.sqrt(diffs * diffs + smooth_sq)
    return slopes[:-1] - slopes[1:]


def per_device(volume, sinogram, ray_mats, offsets, ray_lists, owner_map):
    rows = volume.shape[0]
    me = lax.axis_index("xy").astype(jnp.int32).reshape(1)
    outgoing = project(me, ray_lists, owner_map, offsets, volume, ray_mats)
    arrived = jnp.sum(exchange(outgoing, NEAR), axis=0)
    values = arrived[: PAIRS * rows].reshape(PAIRS, rows, W)
    sums = arrived[PAIRS * rows : PAIRS * rows + PAIRS].reshape(PAIRS, 1, W)
    outgoing = jnp.concatenate([values, jnp.pad(sums, ((0, 0), (0, 7), (0, 0)))], axis=1)
    arrived = jnp.sum(exchange(outgoing, FAR), axis=0)
    weighted = (sinogram - arrived[:rows]) / arrived[rows : rows + 1]
    spread = jnp.broadcast_to(weighted[None], (PAIRS, rows, W))
    column = exchange(spread, FAR)
    spread = jnp.broadcast_to(column[None], (2 * NX, PAIRS, rows, W))
    got = exchange(spread, NEAR)
    base = volume - tv_weight * total_variation(with_faces(volume))
    new_volume = back_project(me, ray_lists, owner_map, offsets, base, ray_mats, got)
    return (new_volume, weighted)


def solution(mesh):
    in_specs = (P("gz", "xy"), P("gz", "xy"), P("xy", None, None, None), P("xy", None), P(), P())
    out_specs = (P("gz", "xy"), P("gz", "xy"))
    return jax.shard_map(
        per_device, mesh=mesh, in_specs=in_specs, out_specs=out_specs, check_vma=False
    )
```

```python
import functools

import jax
import jax.numpy as jnp
from jax import lax
from jax.experimental import pallas as pl
from jax.experimental.pallas import tpu as pltpu
from jax.sharding import PartitionSpec as P

relax = 1.0
tv_weight = 0.2
smooth_sq = 0.01

NX, NY = 4, 8
PAIRS = NY // 2
NEAR_SIZE = 2 * NX
W = 256
LANES = 128
HALVES = 2
FAR_STEPS = (1, 3, 2)
VMEM_LIMIT = 40 * 1024 * 1024
VMEM_MOST = 60 * 1024 * 1024


def device_of(pair, odd, x):
    return (2 * (pair % PAIRS) + odd) * NX + x


NEAR = [[device_of(p, q, x) for q in range(2) for x in range(NX)] for p in range(PAIRS)]


def near_exchange(value):
    return lax.all_to_all(
        value, "xy", split_axis=0, concat_axis=0, axis_index_groups=NEAR, tiled=True
    )


def far_send(value, step):
    moves = [
        (device_of(p, q, x), device_of(p + step, q, x))
        for p in range(PAIRS)
        for q in range(2)
        for x in range(NX)
    ]
    return lax.ppermute(value, "xy", moves)


def split3(value):
    high = value.astype(jnp.bfloat16)
    rest = value - high.astype(jnp.float32)
    mid = rest.astype(jnp.bfloat16)
    low = (rest - mid.astype(jnp.float32)).astype(jnp.bfloat16)
    return [high, mid, low]


def with_ones(value):
    ones = jnp.ones((16, value.shape[1]), jnp.bfloat16)
    return jnp.concatenate(split3(value) + [ones], axis=0)


def join3(product, rows):
    return product[2 * rows : 3 * rows] + product[rows : 2 * rows] + product[:rows]


def near_far(owner, me, sign):
    y, x = owner // NX, owner % NX
    apart = sign * (y // 2 - me // (2 * NX)) + PAIRS
    return (y % 2) * NX + x, apart % PAIRS


def fetch_all(pairs, sems):
    copies = [pltpu.make_async_copy(src, dst, sems.at[i]) for i, (src, dst) in enumerate(pairs)]
    for copy in copies:
        copy.start()
    return copies


def project_kernel(
    first, rows, sums, me_ref, lists_hbm, owners_hbm, starts_hbm, vol_hbm, mats_hbm, out_ref,
    lists, owners, starts, wide, mats, sems, mat_sems,
):
    count = mats.shape[0]
    cols = vol_hbm.shape[1]
    small = fetch_all(
        [
            (lists_hbm, lists),
            (owners_hbm, owners),
            (starts_hbm, starts),
            (vol_hbm.at[pl.ds(first, rows)], wide.at[:, pl.ds(0, cols)]),
        ],
        sems,
    )
    big = fetch_all([(mats_hbm.at[0, k], mats.at[k]) for k in range(count)], mat_sems)
    out_ref[...] = jnp.zeros(out_ref.shape, jnp.float32)
    wide[:, cols:] = jnp.zeros((rows, LANES), jnp.float32)
    for copy in small:
        copy.wait()
    me = me_ref[0]
    for k in range(count):
        start = starts[0, k]
        near, far = near_far(owners[0, lists[k, me]], me, 1)
        base = pl.multiple_of((start // LANES) * LANES, LANES)
        window = wide[:, pl.ds(base, W + LANES)]
        window = pltpu.roll(window, (W + LANES) - start % LANES, 1)[:, :W]
        left = with_ones(window)
        big[k].wait()
        product = jnp.dot(left, mats[k], preferred_element_type=jnp.float32)
        out_ref[near, pl.ds(pl.multiple_of(far * rows, 8), rows), :] = join3(product, rows)
        if sums:
            out_ref[near, pl.ds(PAIRS * rows + far, 1), :] = product[3 * rows : 3 * rows + 1]


HBM = pl.BlockSpec(memory_space=pl.ANY)
SMEM = pl.BlockSpec(memory_space=pltpu.SMEM)
VMEM = pl.BlockSpec(memory_space=pltpu.VMEM)


def small_scratch(lists, owners, starts):
    return [pltpu.SMEM(a.shape, jnp.int32) for a in (lists, owners, starts)]


def project(first, rows, sums, me, lists, owners, starts, volume, mats):
    cols = volume.shape[1]
    count = mats.shape[1]
    out_rows = PAIRS * rows + (8 if sums else 0)
    return pl.pallas_call(
        functools.partial(project_kernel, first, rows, sums),
        out_shape=jax.ShapeDtypeStruct((NEAR_SIZE, out_rows, W), jnp.float32),
        in_specs=[SMEM] + [HBM] * 5,
        out_specs=VMEM,
        scratch_shapes=small_scratch(lists, owners, starts)
        + [
            pltpu.VMEM((rows, cols + LANES), jnp.float32),
            pltpu.VMEM(mats.shape[1:], jnp.bfloat16),
            pltpu.SemaphoreType.DMA((4,)),
            pltpu.SemaphoreType.DMA((count,)),
        ],
        compiler_params=pltpu.CompilerParams(vmem_limit_bytes=VMEM_MOST if sums else VMEM_LIMIT),
        cost_estimate=pl.CostEstimate(
            flops=2 * 3 * count * rows * W * W, bytes_accessed=6 << 20, transcendentals=0
        ),
    )(me, lists, owners, starts, volume, mats)


def gather_kernel(rows, sums, in_ref, *outs):
    outs = outs[-PAIRS:]
    total = in_ref[0]
    for i in range(1, NEAR_SIZE):
        total = total + in_ref[i]
    for far in range(PAIRS):
        outs[far][:rows] = total[far * rows : (far + 1) * rows]
        if sums:
            outs[far][rows:] = jnp.broadcast_to(
                total[PAIRS * rows + far : PAIRS * rows + far + 1], (8, W)
            )


def gather_near(rows, sums, arrived, after):
    out = jax.ShapeDtypeStruct((rows + (8 if sums else 0), W), jnp.float32)
    return pl.pallas_call(
        functools.partial(gather_kernel, rows, sums),
        out_shape=[out] * PAIRS,
        in_specs=[VMEM] + [HBM] * len(after),
        out_specs=[VMEM] * PAIRS,
        compiler_params=pltpu.CompilerParams(vmem_limit_bytes=VMEM_LIMIT),
    )(arrived, *after)


def spread_kernel(*refs):
    parts = refs[:PAIRS]
    out_hbm, token_ref, column, sems = refs[PAIRS:]
    for far in range(PAIRS):
        column[far] = parts[far][...]
    copies = fetch_all([(column, out_hbm.at[i]) for i in range(NEAR_SIZE)], sems)
    token_ref[...] = column[0, :8, :LANES]
    for copy in copies:
        copy.wait()


def spread_near(parts):
    rows = parts[0].shape[0]
    return pl.pallas_call(
        spread_kernel,
        out_shape=[
            jax.ShapeDtypeStruct((NEAR_SIZE, PAIRS, rows, W), jnp.float32),
            jax.ShapeDtypeStruct((8, LANES), jnp.float32),
        ],
        in_specs=[VMEM] * PAIRS,
        out_specs=[HBM, VMEM],
        scratch_shapes=[
            pltpu.VMEM((PAIRS, rows, W), jnp.float32),
            pltpu.SemaphoreType.DMA((NEAR_SIZE,)),
        ],
        compiler_params=pltpu.CompilerParams(vmem_limit_bytes=VMEM_LIMIT),
    )(*parts)


def back_kernel(
    first, rows, has_old, me_ref, lists_hbm, owners_hbm, starts_hbm, base_hbm, mats_hbm, got_ref, *rest
):
    if has_old:
        rest = rest[1:]
    out_hbm, lists, owners, starts, base_v, mats, total, result, sems, mat_sems, out_sem = rest
    count = mats.shape[0]
    cols = base_hbm.shape[1]
    small = fetch_all(
        [
            (lists_hbm, lists),
            (owners_hbm, owners),
            (starts_hbm, starts),
            (base_hbm.at[pl.ds(first, rows)], base_v),
        ],
        sems,
    )
    big = fetch_all([(mats_hbm.at[0, k], mats.at[k]) for k in range(count)], mat_sems)
    total[...] = jnp.zeros(total.shape, jnp.float32)
    for copy in small:
        copy.wait()
    me = me_ref[0]
    for k in range(count):
        start = starts[0, k]
        near, far = near_far(owners[0, lists[k, me]], me, -1)
        base = pl.multiple_of((start // LANES) * LANES, LANES)
        left = with_ones(got_ref[near, far])
        big[k].wait()
        product = lax.dot_general(
            left, mats[k], (((1,), (1,)), ((), ())), preferred_element_type=jnp.float32
        )
        value = jnp.concatenate([join3(product, rows), product[3 * rows : 3 * rows + 8]], axis=0)
        value = jnp.concatenate([value, jnp.zeros((rows + 8, LANES), jnp.float32)], axis=1)
        total[:, pl.ds(base, W + LANES)] += pltpu.roll(value, start % LANES, 1)
    column = jnp.maximum(total[rows : rows + 1, :cols], 1.0)
    result[...] = base_v[...] + relax * (total[:rows, :cols] / column)
    out = pltpu.make_async_copy(result, out_hbm.at[pl.ds(first, rows)], out_sem.at[0])
    out.start()
    out.wait()


def back_project(first, rows, old, me, lists, owners, starts, base, mats, got):
    cols = base.shape[1]
    count = mats.shape[1]
    more = [] if old is None else [old]
    return pl.pallas_call(
        functools.partial(back_kernel, first, rows, bool(more)),
        out_shape=jax.ShapeDtypeStruct(base.shape, jnp.float32),
        in_specs=[SMEM] + [HBM] * 5 + [VMEM] + [HBM] * len(more),
        out_specs=HBM,
        scratch_shapes=small_scratch(lists, owners, starts)
        + [
            pltpu.VMEM((rows, cols), jnp.float32),
            pltpu.VMEM(mats.shape[1:], jnp.bfloat16),
            pltpu.VMEM((rows + 8, cols + LANES), jnp.float32),
            pltpu.VMEM((rows, cols), jnp.float32),
            pltpu.SemaphoreType.DMA((4,)),
            pltpu.SemaphoreType.DMA((count,)),
            pltpu.SemaphoreType.DMA((1,)),
        ],
        input_output_aliases={7: 0} if more else {},
        compiler_params=pltpu.CompilerParams(vmem_limit_bytes=VMEM_LIMIT),
        cost_estimate=pl.CostEstimate(
            flops=2 * 3 * count * rows * W * W, bytes_accessed=6 << 20, transcendentals=0
        ),
    )(me, lists, owners, starts, base, mats, got, *more)


def with_faces(volume):
    count = lax.axis_size("gz")
    up = [(i, i + 1) for i in range(count - 1)]
    down = [(i + 1, i) for i in range(count - 1)]
    return jnp.concatenate(
        [
            lax.ppermute(volume[-1:], "gz", up),
            volume,
            lax.ppermute(volume[:1], "gz", down),
        ],
        axis=0,
    )


def total_variation(padded):
    diffs = padded[1:] - padded[:-1]
    slopes = diffs / jnp.sqrt(diffs * diffs + smooth_sq)
    return slopes[:-1] - slopes[1:]


def per_device(volume, sinogram, ray_mats, offsets, ray_lists, owner_map):
    rows = volume.shape[0] // HALVES
    me = lax.axis_index("xy").astype(jnp.int32).reshape(1)
    common = (me, ray_lists.T, owner_map.reshape(1, -1), offsets)
    arrived = [
        near_exchange(project(h * rows, rows, h == 0, *common, volume, ray_mats))
        for h in range(HALVES)
    ]
    rowsum = None
    weighted = []
    got = []
    spreads = []
    for h in range(HALVES):
        parts = gather_near(rows, h == 0, arrived[h], spreads)
        total = parts[0] + sum(far_send(parts[step], step) for step in FAR_STEPS)
        if h == 0:
            rowsum = total[rows : rows + 1]
        mine = (sinogram[h * rows : (h + 1) * rows] - total[:rows]) / rowsum
        weighted.append(mine)
        far = {0: mine, **{step: far_send(mine, step) for step in FAR_STEPS}}
        spread, token = spread_near([far[i] for i in range(PAIRS)])
        spreads.append(token)
        got.append(near_exchange(spread))
    base = volume - tv_weight * total_variation(with_faces(volume))
    new_volume = None
    for h in range(HALVES):
        new_volume = back_project(h * rows, rows, new_volume, *common, base, ray_mats, got[h])
    return (new_volume, jnp.concatenate(weighted, axis=0))


def solution(mesh):
    in_specs = (P("gz", "xy"), P("gz", "xy"), P("xy", None, None, None), P("xy", None), P(), P())
    out_specs = (P("gz", "xy"), P("gz", "xy"))
    return jax.shard_map(
        per_device, mesh=mesh, in_specs=in_specs, out_specs=out_specs, check_vma=False
    )
```

```python
import functools

import jax
import jax.numpy as jnp
from jax import lax
from jax.experimental import pallas as pl
from jax.experimental.pallas import tpu as pltpu
from jax.sharding import PartitionSpec as P

relax = 1.0
tv_weight = 0.2
smooth_sq = 0.01

NX, NY = 4, 8
PAIRS = NY // 2
NEAR_SIZE = 2 * NX
W = 256
LANES = 128
HALVES = 1
FAR_STEPS = (1, 3, 2)
VMEM_LIMIT = 40 * 1024 * 1024
VMEM_MOST = 60 * 1024 * 1024
VMEM_SPREAD = 52 * 1024 * 1024
VMEM_BACK = 50 * 1024 * 1024


def device_of(pair, odd, x):
    return (2 * (pair % PAIRS) + odd) * NX + x


NEAR = [[device_of(p, q, x) for q in range(2) for x in range(NX)] for p in range(PAIRS)]


def near_exchange(value):
    return lax.all_to_all(
        value, "xy", split_axis=0, concat_axis=0, axis_index_groups=NEAR, tiled=True
    )


def far_send(value, step):
    moves = [
        (device_of(p, q, x), device_of(p + step, q, x))
        for p in range(PAIRS)
        for q in range(2)
        for x in range(NX)
    ]
    return lax.ppermute(value, "xy", moves)


def split3(value):
    high = value.astype(jnp.bfloat16)
    rest = value - high.astype(jnp.float32)
    mid = rest.astype(jnp.bfloat16)
    low = (rest - mid.astype(jnp.float32)).astype(jnp.bfloat16)
    return [high, mid, low]


def with_ones(value):
    ones = jnp.ones((16, value.shape[1]), jnp.bfloat16)
    return jnp.concatenate(split3(value) + [ones], axis=0)


def join3(product, rows):
    return product[2 * rows : 3 * rows] + product[rows : 2 * rows] + product[:rows]


def near_far(owner, me, sign):
    y, x = owner // NX, owner % NX
    apart = sign * (y // 2 - me // (2 * NX)) + PAIRS
    return (y % 2) * NX + x, apart % PAIRS


def fetch_all(pairs, sems):
    copies = [pltpu.make_async_copy(src, dst, sems.at[i]) for i, (src, dst) in enumerate(pairs)]
    for copy in copies:
        copy.start()
    return copies


def mat_copy(mats_hbm, mats, sems, k):
    return pltpu.make_async_copy(mats_hbm.at[0, k], mats.at[k], sems.at[k])


def start_mats(mats_hbm, mats, sems):
    for k in range(mats.shape[0]):
        mat_copy(mats_hbm, mats, sems, k).start()


def project_kernel(
    first, rows, sums, me_ref, lists_hbm, owners_hbm, starts_hbm, vol_hbm, mats_hbm, out_ref,
    lists, owners, starts, wide, mats, sems, mat_sems,
):
    count = mats.shape[0]
    cols = vol_hbm.shape[1]
    small = fetch_all(
        [
            (lists_hbm, lists),
            (owners_hbm, owners),
            (starts_hbm, starts),
            (vol_hbm.at[pl.ds(first, rows)], wide.at[:, pl.ds(0, cols)]),
        ],
        sems,
    )
    start_mats(mats_hbm, mats, mat_sems)
    out_ref[...] = jnp.zeros(out_ref.shape, jnp.float32)
    wide[:, cols:] = jnp.zeros((rows, LANES), jnp.float32)
    for copy in small:
        copy.wait()
    me = me_ref[0]

    def step(k, carry):
        start = starts[0, k]
        near, far = near_far(owners[0, lists[k, me]], me, 1)
        base = pl.multiple_of((start // LANES) * LANES, LANES)
        window = wide[:, pl.ds(base, W + LANES)]
        window = pltpu.roll(window, (W + LANES) - start % LANES, 1)[:, :W]
        left = with_ones(window)
        mat_copy(mats_hbm, mats, mat_sems, k).wait()
        product = jnp.dot(left, mats[k], preferred_element_type=jnp.float32)
        out_ref[near, pl.ds(pl.multiple_of(far * rows, 8), rows), :] = join3(product, rows)
        if sums:
            out_ref[near, pl.ds(PAIRS * rows + far, 1), :] = product[3 * rows : 3 * rows + 1]
        return carry

    lax.fori_loop(0, count, step, 0, unroll=2)


HBM = pl.BlockSpec(memory_space=pl.ANY)
SMEM = pl.BlockSpec(memory_space=pltpu.SMEM)
VMEM = pl.BlockSpec(memory_space=pltpu.VMEM)


def small_scratch(lists, owners, starts):
    return [pltpu.SMEM(a.shape, jnp.int32) for a in (lists, owners, starts)]


def project(first, rows, sums, me, lists, owners, starts, volume, mats):
    cols = volume.shape[1]
    count = mats.shape[1]
    out_rows = PAIRS * rows + (8 if sums else 0)
    return pl.pallas_call(
        functools.partial(project_kernel, first, rows, sums),
        out_shape=jax.ShapeDtypeStruct((NEAR_SIZE, out_rows, W), jnp.float32),
        in_specs=[SMEM] + [HBM] * 5,
        out_specs=VMEM,
        scratch_shapes=small_scratch(lists, owners, starts)
        + [
            pltpu.VMEM((rows, cols + LANES), jnp.float32),
            pltpu.VMEM(mats.shape[1:], jnp.bfloat16),
            pltpu.SemaphoreType.DMA((4,)),
            pltpu.SemaphoreType.DMA((count,)),
        ],
        compiler_params=pltpu.CompilerParams(vmem_limit_bytes=VMEM_MOST if sums else VMEM_LIMIT),
        cost_estimate=pl.CostEstimate(
            flops=2 * 3 * count * rows * W * W, bytes_accessed=6 << 20, transcendentals=0
        ),
    )(me, lists, owners, starts, volume, mats)


def gather_kernel(rows, sums, in_ref, *outs):
    outs = outs[-PAIRS:]
    total = in_ref[0]
    for i in range(1, NEAR_SIZE):
        total = total + in_ref[i]
    for far in range(PAIRS):
        outs[far][:rows] = total[far * rows : (far + 1) * rows]
        if sums:
            outs[far][rows:] = jnp.broadcast_to(
                total[PAIRS * rows + far : PAIRS * rows + far + 1], (8, W)
            )


def gather_near(rows, sums, arrived, after):
    out = jax.ShapeDtypeStruct((rows + (8 if sums else 0), W), jnp.float32)
    return pl.pallas_call(
        functools.partial(gather_kernel, rows, sums),
        out_shape=[out] * PAIRS,
        in_specs=[VMEM] + [HBM] * len(after),
        out_specs=[VMEM] * PAIRS,
        compiler_params=pltpu.CompilerParams(vmem_limit_bytes=VMEM_LIMIT),
    )(arrived, *after)


def spread_kernel(*refs):
    parts = refs[:PAIRS]
    out_hbm, token_ref, column, sems = refs[PAIRS:]
    for far in range(PAIRS):
        column[far] = parts[far][...]
    copies = fetch_all([(column, out_hbm.at[i]) for i in range(NEAR_SIZE)], sems)
    token_ref[...] = column[0, :8, :LANES]
    for copy in copies:
        copy.wait()


def spread_near(parts):
    rows = parts[0].shape[0]
    return pl.pallas_call(
        spread_kernel,
        out_shape=[
            jax.ShapeDtypeStruct((NEAR_SIZE, PAIRS, rows, W), jnp.float32),
            jax.ShapeDtypeStruct((8, LANES), jnp.float32),
        ],
        in_specs=[VMEM] * PAIRS,
        out_specs=[HBM, VMEM],
        scratch_shapes=[
            pltpu.VMEM((PAIRS, rows, W), jnp.float32),
            pltpu.SemaphoreType.DMA((NEAR_SIZE,)),
        ],
        compiler_params=pltpu.CompilerParams(vmem_limit_bytes=VMEM_SPREAD),
    )(*parts)


def back_kernel(
    first, rows, has_old, me_ref, lists_hbm, owners_hbm, starts_hbm, base_hbm, mats_hbm, got_hbm, *rest
):
    if has_old:
        rest = rest[1:]
    out_hbm, lists, owners, starts, base_v, mats, got, total, result, sems, mat_sems, got_sems, out_sem = rest
    count = mats.shape[0]
    cols = base_hbm.shape[1]
    small = fetch_all(
        [
            (lists_hbm, lists),
            (owners_hbm, owners),
            (starts_hbm, starts),
            (base_hbm.at[pl.ds(first, rows)], base_v),
        ],
        sems,
    )
    start_mats(mats_hbm, mats, mat_sems)
    total[...] = jnp.zeros(total.shape, jnp.float32)
    for copy in small[:-1]:
        copy.wait()
    me = me_ref[0]

    def got_copy(k):
        near, far = near_far(owners[0, lists[k, me]], me, -1)
        return pltpu.make_async_copy(got_hbm.at[near, far], got.at[k], got_sems.at[k])

    for k in range(count):
        got_copy(k).start()

    def step(k, carry):
        start = starts[0, k]
        base = pl.multiple_of((start // LANES) * LANES, LANES)
        got_copy(k).wait()
        left = with_ones(got[k])
        mat_copy(mats_hbm, mats, mat_sems, k).wait()
        product = lax.dot_general(
            left, mats[k], (((1,), (1,)), ((), ())), preferred_element_type=jnp.float32
        )
        value = jnp.concatenate([join3(product, rows), product[3 * rows : 3 * rows + 8]], axis=0)
        value = jnp.concatenate([value, jnp.zeros((rows + 8, LANES), jnp.float32)], axis=1)
        total[:, pl.ds(base, W + LANES)] += pltpu.roll(value, start % LANES, 1)
        return carry

    lax.fori_loop(0, count, step, 0, unroll=2)
    small[-1].wait()
    column = jnp.maximum(total[rows : rows + 1, :cols], 1.0)
    result[...] = base_v[...] + relax * (total[:rows, :cols] / column)
    out = pltpu.make_async_copy(result, out_hbm.at[pl.ds(first, rows)], out_sem.at[0])
    out.start()
    out.wait()


def back_project(first, rows, old, me, lists, owners, starts, base, mats, got):
    cols = base.shape[1]
    count = mats.shape[1]
    more = [] if old is None else [old]
    return pl.pallas_call(
        functools.partial(back_kernel, first, rows, bool(more)),
        out_shape=jax.ShapeDtypeStruct(base.shape, jnp.float32),
        in_specs=[SMEM] + [HBM] * (6 + len(more)),
        out_specs=HBM,
        scratch_shapes=small_scratch(lists, owners, starts)
        + [
            pltpu.VMEM((rows, cols), jnp.float32),
            pltpu.VMEM(mats.shape[1:], jnp.bfloat16),
            pltpu.VMEM((count, rows, W), jnp.float32),
            pltpu.VMEM((rows + 8, cols + LANES), jnp.float32),
            pltpu.VMEM((rows, cols), jnp.float32),
            pltpu.SemaphoreType.DMA((4,)),
            pltpu.SemaphoreType.DMA((count,)),
            pltpu.SemaphoreType.DMA((count,)),
            pltpu.SemaphoreType.DMA((1,)),
        ],
        input_output_aliases={7: 0} if more else {},
        compiler_params=pltpu.CompilerParams(vmem_limit_bytes=VMEM_BACK),
        cost_estimate=pl.CostEstimate(
            flops=2 * 3 * count * rows * W * W, bytes_accessed=6 << 20, transcendentals=0
        ),
    )(me, lists, owners, starts, base, mats, got, *more)


def with_faces(volume):
    count = lax.axis_size("gz")
    up = [(i, i + 1) for i in range(count - 1)]
    down = [(i + 1, i) for i in range(count - 1)]
    return jnp.concatenate(
        [
            lax.ppermute(volume[-1:], "gz", up),
            volume,
            lax.ppermute(volume[:1], "gz", down),
        ],
        axis=0,
    )


def total_variation(padded):
    diffs = padded[1:] - padded[:-1]
    slopes = diffs / jnp.sqrt(diffs * diffs + smooth_sq)
    return slopes[:-1] - slopes[1:]


def per_device(volume, sinogram, ray_mats, offsets, ray_lists, owner_map):
    rows = volume.shape[0] // HALVES
    me = lax.axis_index("xy").astype(jnp.int32).reshape(1)
    common = (me, ray_lists.T, owner_map.reshape(1, -1), offsets)
    arrived = [
        near_exchange(project(h * rows, rows, h == 0, *common, volume, ray_mats))
        for h in range(HALVES)
    ]
    rowsum = None
    weighted = []
    got = []
    spreads = []
    for h in range(HALVES):
        parts = gather_near(rows, h == 0, arrived[h], spreads)
        total = parts[0] + sum(far_send(parts[step], step) for step in FAR_STEPS)
        if h == 0:
            rowsum = total[rows : rows + 1]
        mine = (sinogram[h * rows : (h + 1) * rows] - total[:rows]) / rowsum
        weighted.append(mine)
        far = {0: mine, **{step: far_send(mine, step) for step in FAR_STEPS}}
        spread, token = spread_near([far[i] for i in range(PAIRS)])
        spreads.append(token)
        got.append(near_exchange(spread))
    base = volume - tv_weight * total_variation(with_faces(volume))
    new_volume = None
    for h in range(HALVES):
        new_volume = back_project(h * rows, rows, new_volume, *common, base, ray_mats, got[h])
    return (new_volume, jnp.concatenate(weighted, axis=0))


def solution(mesh):
    in_specs = (P("gz", "xy"), P("gz", "xy"), P("xy", None, None, None), P("xy", None), P(), P())
    out_specs = (P("gz", "xy"), P("gz", "xy"))
    return jax.shard_map(
        per_device, mesh=mesh, in_specs=in_specs, out_specs=out_specs, check_vma=False
    )
```

```python
import functools

import jax
import jax.numpy as jnp
from jax import lax
from jax.experimental import pallas as pl
from jax.experimental.pallas import tpu as pltpu
from jax.sharding import PartitionSpec as P

relax = 1.0
tv_weight = 0.2
smooth_sq = 0.01

NX, NY = 4, 8
PAIRS = NY // 2
NEAR_SIZE = 2 * NX
W = 256
LANES = 128
VMEM_LIMIT = 32 * 1024 * 1024


def device_of(pair, odd, x):
    return (2 * pair + odd) * NX + x


NEAR = [[device_of(p, q, x) for q in range(2) for x in range(NX)] for p in range(PAIRS)]
FAR = [[device_of(p, q, x) for p in range(PAIRS)] for q in range(2) for x in range(NX)]


def exchange(value, groups):
    return lax.all_to_all(
        value, "xy", split_axis=0, concat_axis=0, axis_index_groups=groups, tiled=True
    )


def split3(value):
    high = value.astype(jnp.bfloat16)
    rest = value - high.astype(jnp.float32)
    mid = rest.astype(jnp.bfloat16)
    low = (rest - mid.astype(jnp.float32)).astype(jnp.bfloat16)
    return [high, mid, low]


def with_ones(value):
    ones = jnp.ones((16, value.shape[1]), jnp.bfloat16)
    return jnp.concatenate(split3(value) + [ones], axis=0)


def near_far(owner):
    y, x = owner // NX, owner % NX
    return (y % 2) * NX + x, y // 2


def join3(product, rows):
    return product[2 * rows : 3 * rows] + product[rows : 2 * rows] + product[:rows]


def fetch_all(pairs, sems):
    copies = [pltpu.make_async_copy(src, dst, sems.at[i]) for i, (src, dst) in enumerate(pairs)]
    for copy in copies:
        copy.start()
    return copies


def pinned(value, space):
    return pltpu.with_memory_space_constraint(value, space)


ANY = pl.BlockSpec(memory_space=pl.ANY)
SMEM = pl.BlockSpec(memory_space=pltpu.SMEM)
VMEM = pl.BlockSpec(memory_space=pltpu.VMEM)
PARAMS = pltpu.CompilerParams(vmem_limit_bytes=VMEM_LIMIT)


def small_scratch(lists, owners, starts):
    return [pltpu.SMEM(a.shape, jnp.int32) for a in (lists, owners, starts)]


def project_kernel(
    me_ref, lists_hbm, owners_hbm, starts_hbm, vol_hbm, mats_hbm, out_ref, mats_ref,
    lists, owners, starts, wide, sems,
):
    rows, cols = vol_hbm.shape
    count = mats_ref.shape[0]
    copies = fetch_all(
        [
            (lists_hbm, lists),
            (owners_hbm, owners),
            (starts_hbm, starts),
            (vol_hbm, wide.at[:, pl.ds(0, cols)]),
            (mats_hbm.at[0], mats_ref),
        ],
        sems,
    )
    wide[:, cols:] = jnp.zeros((rows, LANES), jnp.float32)
    out_ref[...] = jnp.zeros(out_ref.shape, jnp.float32)
    for copy in copies:
        copy.wait()
    me = me_ref[0]
    for k in range(count):
        start = starts[0, k]
        near, far = near_far(owners[0, lists[k, me]])
        base = pl.multiple_of((start // LANES) * LANES, LANES)
        window = wide[:, pl.ds(base, W + LANES)]
        window = pltpu.roll(window, (W + LANES) - start % LANES, 1)[:, :W]
        product = jnp.dot(with_ones(window), mats_ref[k], preferred_element_type=jnp.float32)
        out_ref[near, pl.ds(pl.multiple_of(far * rows, 8), rows), :] = join3(product, rows)
        out_ref[near, pl.ds(PAIRS * rows + far, 1), :] = product[3 * rows : 3 * rows + 1]


def project(me, lists, owners, starts, volume, mats):
    rows, cols = volume.shape
    operands = [pinned(a, pltpu.HBM) for a in (lists, owners, starts, volume, mats)]
    return pl.pallas_call(
        project_kernel,
        out_shape=[
            pltpu.VMEM((NEAR_SIZE, PAIRS * rows + 8, W), jnp.float32),
            pltpu.VMEM(mats.shape[1:], jnp.bfloat16),
        ],
        in_specs=[SMEM] + [ANY] * 5,
        out_specs=[VMEM, VMEM],
        scratch_shapes=small_scratch(lists, owners, starts)
        + [pltpu.VMEM((rows, cols + LANES), jnp.float32), pltpu.SemaphoreType.DMA((5,))],
        compiler_params=PARAMS,
    )(me, *operands)


def gather_kernel(rows, in_ref, vol_hbm, out_ref, first_ref, last_ref, ends, sems):
    height = vol_hbm.shape[0]
    copies = fetch_all(
        [
            (vol_hbm.at[pl.ds(0, 8)], ends.at[0]),
            (vol_hbm.at[pl.ds(height - 8, 8)], ends.at[1]),
        ],
        sems,
    )
    total = in_ref[0]
    for i in range(1, NEAR_SIZE):
        total = total + in_ref[i]
    for far in range(PAIRS):
        out_ref[far, :rows] = total[far * rows : (far + 1) * rows]
        out_ref[far, rows:] = jnp.broadcast_to(
            total[PAIRS * rows + far : PAIRS * rows + far + 1], (8, W)
        )
    for copy in copies:
        copy.wait()
    first_ref[...] = ends[0, :1]
    last_ref[...] = ends[1, 7:]


def gather_near(arrived, volume):
    rows, cols = volume.shape
    face = jax.ShapeDtypeStruct((1, cols), jnp.float32)
    return pl.pallas_call(
        functools.partial(gather_kernel, rows),
        out_shape=[jax.ShapeDtypeStruct((PAIRS, rows + 8, W), jnp.float32), face, face],
        in_specs=[VMEM, ANY],
        out_specs=[VMEM] * 3,
        scratch_shapes=[pltpu.VMEM((2, 8, cols), jnp.float32), pltpu.SemaphoreType.DMA((2,))],
        compiler_params=PARAMS,
    )(pinned(arrived, pltpu.VMEM), pinned(volume, pltpu.HBM))


def spread_kernel(column_ref, after_ref, out_ref):
    for i in range(NEAR_SIZE):
        out_ref[i] = column_ref[...]


def spread_near(column, after):
    return pl.pallas_call(
        spread_kernel,
        out_shape=pltpu.VMEM((NEAR_SIZE,) + column.shape, jnp.float32),
        in_specs=[VMEM, ANY],
        out_specs=VMEM,
        compiler_params=PARAMS,
    )(column, after)


def back_kernel(
    me_ref, lists_hbm, owners_hbm, starts_hbm, base_ref, mats_ref, got_ref, out_ref,
    lists, owners, starts, total, sems,
):
    rows, cols = base_ref.shape
    count = mats_ref.shape[0]
    copies = fetch_all([(lists_hbm, lists), (owners_hbm, owners), (starts_hbm, starts)], sems)
    total[...] = jnp.zeros(total.shape, jnp.float32)
    for copy in copies:
        copy.wait()
    me = me_ref[0]
    for k in range(count):
        start = starts[0, k]
        near, far = near_far(owners[0, lists[k, me]])
        base = pl.multiple_of((start // LANES) * LANES, LANES)
        product = lax.dot_general(
            with_ones(got_ref[near, far]),
            mats_ref[k],
            (((1,), (1,)), ((), ())),
            preferred_element_type=jnp.float32,
        )
        value = jnp.concatenate([join3(product, rows), product[3 * rows : 3 * rows + 8]], axis=0)
        value = jnp.concatenate([value, jnp.zeros((rows + 8, LANES), jnp.float32)], axis=1)
        total[:, pl.ds(base, W + LANES)] += pltpu.roll(value, start % LANES, 1)
    column = jnp.maximum(total[rows : rows + 1, :cols], 1.0)
    out_ref[...] = base_ref[...] + relax * (total[:rows, :cols] / column)


def back_project(me, lists, owners, starts, base, mats, got):
    rows, cols = base.shape
    operands = [pinned(a, pltpu.HBM) for a in (lists, owners, starts)]
    operands += [pinned(a, pltpu.VMEM) for a in (base, mats, got)]
    return pl.pallas_call(
        back_kernel,
        out_shape=jax.ShapeDtypeStruct((rows, cols), jnp.float32),
        in_specs=[SMEM] + [ANY] * 3 + [VMEM] * 3,
        out_specs=VMEM,
        scratch_shapes=small_scratch(lists, owners, starts)
        + [pltpu.VMEM((rows + 8, cols + LANES), jnp.float32), pltpu.SemaphoreType.DMA((3,))],
        compiler_params=PARAMS,
    )(me, *operands)


def with_faces(volume, first, last):
    count = lax.axis_size("gz")
    up = [(i, i + 1) for i in range(count - 1)]
    down = [(i + 1, i) for i in range(count - 1)]
    return jnp.concatenate(
        [lax.ppermute(last, "gz", up), volume, lax.ppermute(first, "gz", down)], axis=0
    )


def total_variation(padded):
    diffs = padded[1:] - padded[:-1]
    slopes = diffs / jnp.sqrt(diffs * diffs + smooth_sq)
    return slopes[:-1] - slopes[1:]


def per_device(volume, sinogram, ray_mats, offsets, ray_lists, owner_map):
    rows = volume.shape[0]
    me = lax.axis_index("xy").astype(jnp.int32).reshape(1)
    plan = (me, ray_lists.T, owner_map.reshape(1, -1), offsets)
    outgoing, mats = project(*plan, volume, ray_mats)
    outgoing, first, last = gather_near(exchange(outgoing, NEAR), volume)
    arrived = jnp.sum(exchange(outgoing, FAR), axis=0)
    base = volume - tv_weight * total_variation(with_faces(volume, first, last))
    weighted = (sinogram - arrived[:rows]) / arrived[rows : rows + 1]
    column = exchange(jnp.broadcast_to(weighted[None], (PAIRS, rows, W)), FAR)
    got = exchange(spread_near(column, base), NEAR)
    new_volume = back_project(*plan, base, mats, got)
    return (new_volume, weighted)


def solution(mesh):
    in_specs = (P("gz", "xy"), P("gz", "xy"), P("xy", None, None, None), P("xy", None), P(), P())
    out_specs = (P("gz", "xy"), P("gz", "xy"))
    return jax.shard_map(
        per_device, mesh=mesh, in_specs=in_specs, out_specs=out_specs, check_vma=False
    )
```

```python
import functools

import jax
import jax.numpy as jnp
from jax import lax
from jax.experimental import pallas as pl
from jax.experimental.pallas import tpu as pltpu
from jax.sharding import PartitionSpec as P

relax = 1.0
tv_weight = 0.2
smooth_sq = 0.01

NX, NY = 4, 8
BX, BY = NX // 2, NY // 2
QUAD, SLOTS = 4, BX * BY
ROWS_A = 48
ROWS_B = 24
MATS_AT_ONCE = 4
W = 256
LANES = 128
VMEM_LIMIT = 32 * 1024 * 1024


def device_of(y, x):
    return (y % NY) * NX + x % NX


PARITIES = [(qy, qx) for qy in range(2) for qx in range(2)]
BLOCKS = [(by, bx) for by in range(BY) for bx in range(BX)]
NEAR = [[device_of(2 * by + qy, 2 * bx + qx) for qy, qx in PARITIES] for by, bx in BLOCKS]
FAR = [[device_of(2 * by + qy, 2 * bx + qx) for by, bx in BLOCKS] for qy, qx in PARITIES]
ODD_X = [(device_of(y, x), device_of(y, x + 2 * (x % 2) - 1)) for y in range(NY) for x in range(NX)]
ODD_Y = [(device_of(y, x), device_of(y + 2 * (y % 2) - 1, x)) for y in range(NY) for x in range(NX)]


def swap_x(value):
    return lax.ppermute(value, "xy", ODD_X)


def swap_y(value):
    return lax.ppermute(value, "xy", ODD_Y)


def exchange(value, groups):
    return lax.all_to_all(
        value, "xy", split_axis=0, concat_axis=0, axis_index_groups=groups, tiled=True
    )


def split3(value):
    high = value.astype(jnp.bfloat16)
    rest = value - high.astype(jnp.float32)
    mid = rest.astype(jnp.bfloat16)
    low = (rest - mid.astype(jnp.float32)).astype(jnp.bfloat16)
    return [high, mid, low]


def with_ones(value):
    ones = jnp.ones((16, value.shape[1]), jnp.bfloat16)
    return jnp.concatenate(split3(value) + [ones], axis=0)


def place(owner, me):
    y, x = owner // NX, owner % NX
    my_y, my_x = me // NX, me % NX
    quad = (y % 2) * 2 + x % 2
    slot = (y // 2) * BX + x // 2
    return quad, slot, (x + my_x) % 2, (y + my_y) % 2


def join3(product, rows):
    return product[2 * rows : 3 * rows] + product[rows : 2 * rows] + product[:rows]


def fetch_all(pairs, sems):
    copies = [pltpu.make_async_copy(src, dst, sems.at[i]) for i, (src, dst) in enumerate(pairs)]
    for copy in copies:
        copy.start()
    return copies


def pinned(value, space):
    return pltpu.with_memory_space_constraint(value, space)


ANY = pl.BlockSpec(memory_space=pl.ANY)
SMEM = pl.BlockSpec(memory_space=pltpu.SMEM)
VMEM = pl.BlockSpec(memory_space=pltpu.VMEM)
PARAMS = pltpu.CompilerParams(vmem_limit_bytes=VMEM_LIMIT)


def small_scratch(lists, owners, starts):
    return [pltpu.SMEM(a.shape, jnp.int32) for a in (lists, owners, starts)]


def slot_rows(slot, rows):
    return pl.ds(pl.multiple_of(slot * rows, 8), rows)


def fetch_mats(mats_hbm, mats, sems):
    return fetch_all(
        [
            (mats_hbm.at[0, pl.ds(k, MATS_AT_ONCE)], mats.at[pl.ds(k, MATS_AT_ONCE)])
            for k in range(0, mats.shape[0], MATS_AT_ONCE)
        ],
        sems,
    )


def wait_mats(copies, k):
    if k % MATS_AT_ONCE == 0:
        copies[k // MATS_AT_ONCE].wait()


def mats_scratch(mats, others):
    count = mats.shape[1]
    return [
        pltpu.VMEM(mats.shape[1:], jnp.bfloat16),
        pltpu.SemaphoreType.DMA((others,)),
        pltpu.SemaphoreType.DMA((count // MATS_AT_ONCE,)),
    ]


def project_kernel(
    me_ref, lists_hbm, owners_hbm, starts_hbm, vol_hbm, mats_hbm,
    a_ref, keep1_ref, send1_ref, keep2_ref, send2_ref,
    lists, owners, starts, wide, part1, part2, mats, sems, mat_sems,
):
    rows, cols = vol_hbm.shape
    count = mats.shape[0]
    copies = fetch_all(
        [
            (lists_hbm, lists),
            (owners_hbm, owners),
            (starts_hbm, starts),
            (vol_hbm, wide.at[:, pl.ds(0, cols)]),
        ],
        sems,
    )
    mat_copies = fetch_mats(mats_hbm, mats, mat_sems)
    wide[:, cols:] = jnp.zeros((rows, LANES), jnp.float32)
    for ref in (a_ref, part1, part2):
        ref[...] = jnp.zeros(ref.shape, jnp.float32)
    for copy in copies:
        copy.wait()
    me = me_ref[0]
    for k in range(count):
        start = starts[0, k]
        quad, slot, other_x, other_y = place(owners[0, lists[k, me]], me)
        base = pl.multiple_of((start // LANES) * LANES, LANES)
        window = wide[:, pl.ds(base, W + LANES)]
        window = pltpu.roll(window, (W + LANES) - start % LANES, 1)[:, :W]
        wait_mats(mat_copies, k)
        product = jnp.dot(with_ones(window), mats[k], preferred_element_type=jnp.float32)
        value = join3(product, rows)
        a_ref[quad, slot_rows(slot, ROWS_A), :] = value[:ROWS_A]
        a_ref[quad, pl.ds(SLOTS * ROWS_A + slot, 1), :] = product[3 * rows : 3 * rows + 1]
        b_rows = slot_rows(slot, ROWS_B)
        part1[other_x, other_y, b_rows, :] = value[ROWS_A : ROWS_A + ROWS_B]
        part2[other_y, other_x, b_rows, :] = value[ROWS_A + ROWS_B :]
    keep1_ref[...] = part1[0]
    send1_ref[...] = part1[1]
    keep2_ref[...] = part2[0]
    send2_ref[...] = part2[1]


def project(me, lists, owners, starts, volume, mats):
    rows, cols = volume.shape
    operands = [pinned(a, pltpu.HBM) for a in (lists, owners, starts, volume, mats)]
    half = pltpu.VMEM((2, SLOTS * ROWS_B, W), jnp.float32)
    return pl.pallas_call(
        project_kernel,
        out_shape=[jax.ShapeDtypeStruct((QUAD, SLOTS * ROWS_A + SLOTS, W), jnp.float32)]
        + [half] * 4,
        in_specs=[SMEM] + [ANY] * 5,
        out_specs=[VMEM] * 5,
        scratch_shapes=small_scratch(lists, owners, starts)
        + [pltpu.VMEM((rows, cols + LANES), jnp.float32)]
        + [pltpu.VMEM((2, 2, SLOTS * ROWS_B, W), jnp.float32)] * 2
        + mats_scratch(mats, 4),
        compiler_params=PARAMS,
    )(me, *operands)


def turn_kernel(keep1, came1, keep2, came2, own1, send1, own2, send2):
    own1[...] = keep1[0] + came1[0]
    send1[...] = keep1[1] + came1[1]
    own2[...] = keep2[0] + came2[0]
    send2[...] = keep2[1] + came2[1]


def turn(keep1, came1, keep2, came2):
    return pl.pallas_call(
        turn_kernel,
        out_shape=[pltpu.VMEM((SLOTS * ROWS_B, W), jnp.float32)] * 4,
        in_specs=[VMEM] * 4,
        out_specs=[VMEM] * 4,
        compiler_params=PARAMS,
    )(*(pinned(a, pltpu.VMEM) for a in (keep1, came1, keep2, came2)))


def gather_kernel(a_ref, own1, came1, own2, came2, vol_hbm, out_ref, first_ref, last_ref, ends, sems):
    height = vol_hbm.shape[0]
    copies = fetch_all(
        [
            (vol_hbm.at[pl.ds(0, 8)], ends.at[0]),
            (vol_hbm.at[pl.ds(height - 8, 8)], ends.at[1]),
        ],
        sems,
    )
    total = a_ref[0]
    for i in range(1, QUAD):
        total = total + a_ref[i]
    total1 = own1[...] + came1[...]
    total2 = own2[...] + came2[...]
    for slot in range(SLOTS):
        out_ref[slot, :ROWS_A] = total[slot * ROWS_A : (slot + 1) * ROWS_A]
        b_rows = slice(slot * ROWS_B, (slot + 1) * ROWS_B)
        out_ref[slot, ROWS_A : ROWS_A + ROWS_B] = total1[b_rows]
        out_ref[slot, ROWS_A + ROWS_B : ROWS_A + 2 * ROWS_B] = total2[b_rows]
        at = SLOTS * ROWS_A + slot
        out_ref[slot, ROWS_A + 2 * ROWS_B :] = jnp.broadcast_to(total[at : at + 1], (8, W))
    for copy in copies:
        copy.wait()
    first_ref[...] = ends[0, :1]
    last_ref[...] = ends[1, 7:]


def gather_near(arrived, own1, came1, own2, came2, volume):
    rows, cols = volume.shape
    face = jax.ShapeDtypeStruct((1, cols), jnp.float32)
    return pl.pallas_call(
        gather_kernel,
        out_shape=[pltpu.VMEM((SLOTS, rows + 8, W), jnp.float32), face, face],
        in_specs=[VMEM] * 5 + [ANY],
        out_specs=[VMEM] * 3,
        scratch_shapes=[pltpu.VMEM((2, 8, cols), jnp.float32), pltpu.SemaphoreType.DMA((2,))],
        compiler_params=PARAMS,
    )(arrived, own1, came1, own2, came2, pinned(volume, pltpu.HBM))


def spread_kernel(column_ref, after_ref, a_ref, one_ref, two_ref):
    for slot in range(SLOTS):
        for i in range(QUAD):
            a_ref[i, slot * ROWS_A : (slot + 1) * ROWS_A] = column_ref[slot, :ROWS_A]
        b_rows = slice(slot * ROWS_B, (slot + 1) * ROWS_B)
        one_ref[b_rows] = column_ref[slot, ROWS_A : ROWS_A + ROWS_B]
        two_ref[b_rows] = column_ref[slot, ROWS_A + ROWS_B :]


def spread_near(column, after):
    part = pltpu.VMEM((SLOTS * ROWS_B, W), jnp.float32)
    return pl.pallas_call(
        spread_kernel,
        out_shape=[jax.ShapeDtypeStruct((QUAD, SLOTS * ROWS_A, W), jnp.float32), part, part],
        in_specs=[VMEM, ANY],
        out_specs=[VMEM] * 3,
        compiler_params=PARAMS,
    )(column, after)


def stack_kernel(own1, came1, own2, came2, pair1, pair2):
    pair1[0] = own1[...]
    pair1[1] = came1[...]
    pair2[0] = own2[...]
    pair2[1] = came2[...]


def stack_pairs(own1, came1, own2, came2):
    return pl.pallas_call(
        stack_kernel,
        out_shape=[pltpu.VMEM((2, SLOTS * ROWS_B, W), jnp.float32)] * 2,
        in_specs=[VMEM] * 4,
        out_specs=[VMEM] * 2,
        compiler_params=PARAMS,
    )(*(pinned(a, pltpu.VMEM) for a in (own1, came1, own2, came2)))


def back_kernel(
    me_ref, lists_hbm, owners_hbm, starts_hbm, mats_hbm,
    base_ref, a_ref, own1, came1, own2, came2, out_ref,
    lists, owners, starts, total, part1, part2, mats, sems, mat_sems,
):
    rows, cols = base_ref.shape
    count = mats.shape[0]
    copies = fetch_all([(lists_hbm, lists), (owners_hbm, owners), (starts_hbm, starts)], sems)
    mat_copies = fetch_mats(mats_hbm, mats, mat_sems)
    total[...] = jnp.zeros(total.shape, jnp.float32)
    part1[0] = own1[...]
    part1[1] = came1[...]
    part2[0] = own2[...]
    part2[1] = came2[...]
    for copy in copies:
        copy.wait()
    me = me_ref[0]
    for k in range(count):
        start = starts[0, k]
        quad, slot, other_x, other_y = place(owners[0, lists[k, me]], me)
        base = pl.multiple_of((start // LANES) * LANES, LANES)
        b_rows = slot_rows(slot, ROWS_B)
        needed = jnp.concatenate(
            [
                a_ref[quad, slot_rows(slot, ROWS_A), :],
                part1[other_x, other_y, b_rows, :],
                part2[other_y, other_x, b_rows, :],
            ],
            axis=0,
        )
        wait_mats(mat_copies, k)
        product = lax.dot_general(
            with_ones(needed),
            mats[k],
            (((1,), (1,)), ((), ())),
            preferred_element_type=jnp.float32,
        )
        value = jnp.concatenate([join3(product, rows), product[3 * rows : 3 * rows + 8]], axis=0)
        value = jnp.concatenate([value, jnp.zeros((rows + 8, LANES), jnp.float32)], axis=1)
        total[:, pl.ds(base, W + LANES)] += pltpu.roll(value, start % LANES, 1)
    column = jnp.maximum(total[rows : rows + 1, :cols], 1.0)
    out_ref[...] = base_ref[...] + relax * (total[:rows, :cols] / column)


def back_project(me, lists, owners, starts, base, mats, *parts):
    rows, cols = base.shape
    operands = [pinned(a, pltpu.HBM) for a in (lists, owners, starts, mats)]
    operands += [pinned(a, pltpu.VMEM) for a in (base,) + parts]
    return pl.pallas_call(
        back_kernel,
        out_shape=jax.ShapeDtypeStruct((rows, cols), jnp.float32),
        in_specs=[SMEM] + [ANY] * 4 + [VMEM] * 6,
        out_specs=VMEM,
        scratch_shapes=small_scratch(lists, owners, starts)
        + [pltpu.VMEM((rows + 8, cols + LANES), jnp.float32)]
        + [pltpu.VMEM((2, 2, SLOTS * ROWS_B, W), jnp.float32)] * 2
        + mats_scratch(mats, 3),
        compiler_params=PARAMS,
    )(me, *operands)


def with_faces(volume, first, last):
    count = lax.axis_size("gz")
    up = [(i, i + 1) for i in range(count - 1)]
    down = [(i + 1, i) for i in range(count - 1)]
    return jnp.concatenate(
        [lax.ppermute(last, "gz", up), volume, lax.ppermute(first, "gz", down)], axis=0
    )


def total_variation(padded):
    diffs = padded[1:] - padded[:-1]
    slopes = diffs / jnp.sqrt(diffs * diffs + smooth_sq)
    return slopes[:-1] - slopes[1:]


def per_device(volume, sinogram, ray_mats, offsets, ray_lists, owner_map):
    rows = volume.shape[0]
    me = lax.axis_index("xy").astype(jnp.int32).reshape(1)
    plan = (me, ray_lists.T, owner_map.reshape(1, -1), offsets)
    a, keep1, send1, keep2, send2 = project(*plan, volume, ray_mats)
    own1, send1, own2, send2 = turn(keep1, swap_x(send1), keep2, swap_y(send2))
    a = exchange(a, NEAR)
    outgoing, first, last = gather_near(a, own1, swap_y(send1), own2, swap_x(send2), volume)
    arrived = jnp.sum(exchange(outgoing, FAR), axis=0)
    base = volume - tv_weight * total_variation(with_faces(volume, first, last))
    weighted = (sinogram - arrived[:rows]) / arrived[rows : rows + 1]
    column = exchange(jnp.broadcast_to(weighted[None], (SLOTS, rows, W)), FAR)
    a, own1, own2 = spread_near(column, base)
    pair1, pair2 = stack_pairs(own1, swap_y(own1), own2, swap_x(own2))
    got = (exchange(a, NEAR), pair1, swap_x(pair1), pair2, swap_y(pair2))
    new_volume = back_project(*plan, base, ray_mats, *got)
    return (new_volume, weighted)


def solution(mesh):
    in_specs = (P("gz", "xy"), P("gz", "xy"), P("xy", None, None, None), P("xy", None), P(), P())
    out_specs = (P("gz", "xy"), P("gz", "xy"))
    return jax.shard_map(
        per_device, mesh=mesh, in_specs=in_specs, out_specs=out_specs, check_vma=False
    )
```

```python
import functools

import jax
import jax.numpy as jnp
from jax import lax
from jax.experimental import pallas as pl
from jax.experimental.pallas import tpu as pltpu
from jax.sharding import PartitionSpec as P

relax = 1.0
tv_weight = 0.2
smooth_sq = 0.01

NX, NY = 4, 8
BX, BY = NX // 2, NY // 2
QUAD, SLOTS = 4, BX * BY
ROWS_A = 64
ROWS_B = 32
MATS_AT_ONCE = 4
W = 256
LANES = 128
VMEM_LIMIT = 32 * 1024 * 1024


def device_of(y, x):
    return (y % NY) * NX + x % NX


PARITIES = [(qy, qx) for qy in range(2) for qx in range(2)]
BLOCKS = [(by, bx) for by in range(BY) for bx in range(BX)]
NEAR = [[device_of(2 * by + qy, 2 * bx + qx) for qy, qx in PARITIES] for by, bx in BLOCKS]
FAR = [[device_of(2 * by + qy, 2 * bx + qx) for by, bx in BLOCKS] for qy, qx in PARITIES]
ODD_X = [(device_of(y, x), device_of(y, x + 2 * (x % 2) - 1)) for y in range(NY) for x in range(NX)]
ODD_Y = [(device_of(y, x), device_of(y + 2 * (y % 2) - 1, x)) for y in range(NY) for x in range(NX)]


def swap_x(value):
    return lax.ppermute(value, "xy", ODD_X)


def swap_y(value):
    return lax.ppermute(value, "xy", ODD_Y)


def exchange(value, groups):
    return lax.all_to_all(
        value, "xy", split_axis=0, concat_axis=0, axis_index_groups=groups, tiled=True
    )


def split3(value):
    high = value.astype(jnp.bfloat16)
    rest = value - high.astype(jnp.float32)
    mid = rest.astype(jnp.bfloat16)
    low = (rest - mid.astype(jnp.float32)).astype(jnp.bfloat16)
    return [high, mid, low]


def with_ones(value):
    ones = jnp.ones((16, value.shape[1]), jnp.bfloat16)
    return jnp.concatenate(split3(value) + [ones], axis=0)


def place(owner, me):
    y, x = owner // NX, owner % NX
    my_y, my_x = me // NX, me % NX
    quad = (y % 2) * 2 + x % 2
    slot = (y // 2) * BX + x // 2
    return quad, slot, (x + my_x) % 2, (y + my_y) % 2


def join3(product, rows):
    return product[2 * rows : 3 * rows] + product[rows : 2 * rows] + product[:rows]


def fetch_all(pairs, sems):
    copies = [pltpu.make_async_copy(src, dst, sems.at[i]) for i, (src, dst) in enumerate(pairs)]
    for copy in copies:
        copy.start()
    return copies


def pinned(value, space):
    return pltpu.with_memory_space_constraint(value, space)


ANY = pl.BlockSpec(memory_space=pl.ANY)
SMEM = pl.BlockSpec(memory_space=pltpu.SMEM)
VMEM = pl.BlockSpec(memory_space=pltpu.VMEM)
PARAMS = pltpu.CompilerParams(vmem_limit_bytes=VMEM_LIMIT)


def small_scratch(lists, owners, starts):
    return [pltpu.SMEM(a.shape, jnp.int32) for a in (lists, owners, starts)]


def slot_rows(slot, rows):
    return pl.ds(pl.multiple_of(slot * rows, 8), rows)


def fetch_mats(mats_hbm, mats, sems):
    return fetch_all(
        [
            (mats_hbm.at[0, pl.ds(k, MATS_AT_ONCE)], mats.at[pl.ds(k, MATS_AT_ONCE)])
            for k in range(0, mats.shape[0], MATS_AT_ONCE)
        ],
        sems,
    )


def wait_mats(copies, k):
    if k % MATS_AT_ONCE == 0:
        copies[k // MATS_AT_ONCE].wait()


def mats_scratch(mats, others):
    count = mats.shape[1]
    return [
        pltpu.VMEM(mats.shape[1:], jnp.bfloat16),
        pltpu.SemaphoreType.DMA((others,)),
        pltpu.SemaphoreType.DMA((count // MATS_AT_ONCE,)),
    ]


def project_kernel(
    me_ref, lists_hbm, owners_hbm, starts_hbm, vol_hbm, mats_hbm,
    a_ref, keep_ref, send_ref, lists, owners, starts, wide, part, mats, sems, mat_sems,
):
    rows, cols = vol_hbm.shape
    count = mats.shape[0]
    copies = fetch_all(
        [
            (lists_hbm, lists),
            (owners_hbm, owners),
            (starts_hbm, starts),
            (vol_hbm, wide.at[:, pl.ds(0, cols)]),
        ],
        sems,
    )
    mat_copies = fetch_mats(mats_hbm, mats, mat_sems)
    wide[:, cols:] = jnp.zeros((rows, LANES), jnp.float32)
    for ref in (a_ref, part):
        ref[...] = jnp.zeros(ref.shape, jnp.float32)
    for copy in copies:
        copy.wait()
    me = me_ref[0]
    for k in range(count):
        start = starts[0, k]
        quad, slot, other_x, other_y = place(owners[0, lists[k, me]], me)
        base = pl.multiple_of((start // LANES) * LANES, LANES)
        window = wide[:, pl.ds(base, W + LANES)]
        window = pltpu.roll(window, (W + LANES) - start % LANES, 1)[:, :W]
        wait_mats(mat_copies, k)
        product = jnp.dot(with_ones(window), mats[k], preferred_element_type=jnp.float32)
        value = join3(product, rows)
        a_ref[quad, slot_rows(slot, ROWS_A), :] = value[:ROWS_A]
        a_ref[quad, pl.ds(SLOTS * ROWS_A + slot, 1), :] = product[3 * rows : 3 * rows + 1]
        part[other_x, other_y, slot_rows(slot, ROWS_B), :] = value[ROWS_A:]
    keep_ref[...] = part[0]
    send_ref[...] = part[1]


def project(me, lists, owners, starts, volume, mats):
    rows, cols = volume.shape
    operands = [pinned(a, pltpu.HBM) for a in (lists, owners, starts, volume, mats)]
    half = pltpu.VMEM((2, SLOTS * ROWS_B, W), jnp.float32)
    return pl.pallas_call(
        project_kernel,
        out_shape=[jax.ShapeDtypeStruct((QUAD, SLOTS * ROWS_A + SLOTS, W), jnp.float32)]
        + [half] * 2,
        in_specs=[SMEM] + [ANY] * 5,
        out_specs=[VMEM] * 3,
        scratch_shapes=small_scratch(lists, owners, starts)
        + [pltpu.VMEM((rows, cols + LANES), jnp.float32)]
        + [pltpu.VMEM((2, 2, SLOTS * ROWS_B, W), jnp.float32)]
        + mats_scratch(mats, 4),
        compiler_params=PARAMS,
    )(me, *operands)


def turn_kernel(keep, came, own, send):
    own[...] = keep[0] + came[0]
    send[...] = keep[1] + came[1]


def turn(keep, came):
    return pl.pallas_call(
        turn_kernel,
        out_shape=[pltpu.VMEM((SLOTS * ROWS_B, W), jnp.float32)] * 2,
        in_specs=[VMEM] * 2,
        out_specs=[VMEM] * 2,
        compiler_params=PARAMS,
    )(pinned(keep, pltpu.VMEM), pinned(came, pltpu.VMEM))


def gather_kernel(a_ref, own, came, vol_hbm, out_ref, first_ref, last_ref, ends, sems):
    height = vol_hbm.shape[0]
    copies = fetch_all(
        [
            (vol_hbm.at[pl.ds(0, 8)], ends.at[0]),
            (vol_hbm.at[pl.ds(height - 8, 8)], ends.at[1]),
        ],
        sems,
    )
    total = a_ref[0]
    for i in range(1, QUAD):
        total = total + a_ref[i]
    total_b = own[...] + came[...]
    for slot in range(SLOTS):
        out_ref[slot, :ROWS_A] = total[slot * ROWS_A : (slot + 1) * ROWS_A]
        rows = ROWS_A + ROWS_B
        out_ref[slot, ROWS_A:rows] = total_b[slot * ROWS_B : (slot + 1) * ROWS_B]
        at = SLOTS * ROWS_A + slot
        out_ref[slot, rows:] = jnp.broadcast_to(total[at : at + 1], (8, W))
    for copy in copies:
        copy.wait()
    first_ref[...] = ends[0, :1]
    last_ref[...] = ends[1, 7:]


def gather_near(arrived, own, came, volume):
    rows, cols = volume.shape
    face = jax.ShapeDtypeStruct((1, cols), jnp.float32)
    return pl.pallas_call(
        gather_kernel,
        out_shape=[pltpu.VMEM((SLOTS, rows + 8, W), jnp.float32), face, face],
        in_specs=[VMEM] * 3 + [ANY],
        out_specs=[VMEM] * 3,
        scratch_shapes=[pltpu.VMEM((2, 8, cols), jnp.float32), pltpu.SemaphoreType.DMA((2,))],
        compiler_params=PARAMS,
    )(arrived, own, came, pinned(volume, pltpu.HBM))


def spread_kernel(column_ref, after_ref, a_ref, b_ref):
    for slot in range(SLOTS):
        for i in range(QUAD):
            a_ref[i, slot * ROWS_A : (slot + 1) * ROWS_A] = column_ref[slot, :ROWS_A]
        b_ref[slot * ROWS_B : (slot + 1) * ROWS_B] = column_ref[slot, ROWS_A:]


def spread_near(column, after):
    part = pltpu.VMEM((SLOTS * ROWS_B, W), jnp.float32)
    return pl.pallas_call(
        spread_kernel,
        out_shape=[jax.ShapeDtypeStruct((QUAD, SLOTS * ROWS_A, W), jnp.float32), part],
        in_specs=[VMEM, ANY],
        out_specs=[VMEM] * 2,
        compiler_params=PARAMS,
    )(column, after)


def stack_kernel(own, came, pair):
    pair[0] = own[...]
    pair[1] = came[...]


def stack_pair(own, came):
    return pl.pallas_call(
        stack_kernel,
        out_shape=pltpu.VMEM((2, SLOTS * ROWS_B, W), jnp.float32),
        in_specs=[VMEM] * 2,
        out_specs=VMEM,
        compiler_params=PARAMS,
    )(pinned(own, pltpu.VMEM), pinned(came, pltpu.VMEM))


def back_kernel(
    me_ref, lists_hbm, owners_hbm, starts_hbm, mats_hbm,
    base_ref, a_ref, own, came, out_ref, lists, owners, starts, total, part, mats, sems, mat_sems,
):
    rows, cols = base_ref.shape
    count = mats.shape[0]
    copies = fetch_all([(lists_hbm, lists), (owners_hbm, owners), (starts_hbm, starts)], sems)
    mat_copies = fetch_mats(mats_hbm, mats, mat_sems)
    total[...] = jnp.zeros(total.shape, jnp.float32)
    part[0] = own[...]
    part[1] = came[...]
    for copy in copies:
        copy.wait()
    me = me_ref[0]
    for k in range(count):
        start = starts[0, k]
        quad, slot, other_x, other_y = place(owners[0, lists[k, me]], me)
        base = pl.multiple_of((start // LANES) * LANES, LANES)
        needed = jnp.concatenate(
            [
                a_ref[quad, slot_rows(slot, ROWS_A), :],
                part[other_x, other_y, slot_rows(slot, ROWS_B), :],
            ],
            axis=0,
        )
        wait_mats(mat_copies, k)
        product = lax.dot_general(
            with_ones(needed),
            mats[k],
            (((1,), (1,)), ((), ())),
            preferred_element_type=jnp.float32,
        )
        value = jnp.concatenate([join3(product, rows), product[3 * rows : 3 * rows + 8]], axis=0)
        value = jnp.concatenate([value, jnp.zeros((rows + 8, LANES), jnp.float32)], axis=1)
        total[:, pl.ds(base, W + LANES)] += pltpu.roll(value, start % LANES, 1)
    column = jnp.maximum(total[rows : rows + 1, :cols], 1.0)
    out_ref[...] = base_ref[...] + relax * (total[:rows, :cols] / column)


def back_project(me, lists, owners, starts, base, mats, *parts):
    rows, cols = base.shape
    operands = [pinned(a, pltpu.HBM) for a in (lists, owners, starts, mats)]
    operands += [pinned(a, pltpu.VMEM) for a in (base,) + parts]
    return pl.pallas_call(
        back_kernel,
        out_shape=jax.ShapeDtypeStruct((rows, cols), jnp.float32),
        in_specs=[SMEM] + [ANY] * 4 + [VMEM] * 4,
        out_specs=VMEM,
        scratch_shapes=small_scratch(lists, owners, starts)
        + [pltpu.VMEM((rows + 8, cols + LANES), jnp.float32)]
        + [pltpu.VMEM((2, 2, SLOTS * ROWS_B, W), jnp.float32)]
        + mats_scratch(mats, 3),
        compiler_params=PARAMS,
    )(me, *operands)


def with_faces(volume, first, last):
    count = lax.axis_size("gz")
    up = [(i, i + 1) for i in range(count - 1)]
    down = [(i + 1, i) for i in range(count - 1)]
    return jnp.concatenate(
        [lax.ppermute(last, "gz", up), volume, lax.ppermute(first, "gz", down)], axis=0
    )


def total_variation(padded):
    diffs = padded[1:] - padded[:-1]
    slopes = diffs / jnp.sqrt(diffs * diffs + smooth_sq)
    return slopes[:-1] - slopes[1:]


def per_device(volume, sinogram, ray_mats, offsets, ray_lists, owner_map):
    rows = volume.shape[0]
    me = lax.axis_index("xy").astype(jnp.int32).reshape(1)
    plan = (me, ray_lists.T, owner_map.reshape(1, -1), offsets)
    a, keep, send = project(*plan, volume, ray_mats)
    own, send = turn(keep, swap_x(send))
    outgoing, first, last = gather_near(exchange(a, NEAR), own, swap_y(send), volume)
    arrived = jnp.sum(exchange(outgoing, FAR), axis=0)
    base = volume - tv_weight * total_variation(with_faces(volume, first, last))
    weighted = (sinogram - arrived[:rows]) / arrived[rows : rows + 1]
    column = exchange(jnp.broadcast_to(weighted[None], (SLOTS, rows, W)), FAR)
    a, own = spread_near(column, base)
    pair = stack_pair(own, swap_y(own))
    got = (exchange(a, NEAR), pair, swap_x(pair))
    new_volume = back_project(*plan, base, ray_mats, *got)
    return (new_volume, weighted)


def solution(mesh):
    in_specs = (P("gz", "xy"), P("gz", "xy"), P("xy", None, None, None), P("xy", None), P(), P())
    out_specs = (P("gz", "xy"), P("gz", "xy"))
    return jax.shard_map(
        per_device, mesh=mesh, in_specs=in_specs, out_specs=out_specs, check_vma=False
    )
```

```python
import functools

import jax
import jax.numpy as jnp
from jax import lax
from jax.experimental import pallas as pl
from jax.experimental.pallas import tpu as pltpu
from jax.sharding import PartitionSpec as P

relax = 1.0
tv_weight = 0.2
smooth_sq = 0.01

NX, NY = 4, 8
BX, BY = NX // 2, NY // 2
QUAD, SLOTS = 4, BX * BY
ROWS_A = 48
ROWS_B = 48
MATS_AT_ONCE = 4
W = 256
LANES = 128
VMEM_LIMIT = 32 * 1024 * 1024


def device_of(y, x):
    return (y % NY) * NX + x % NX


PARITIES = [(qy, qx) for qy in range(2) for qx in range(2)]
BLOCKS = [(by, bx) for by in range(BY) for bx in range(BX)]
NEAR = [[device_of(2 * by + qy, 2 * bx + qx) for qy, qx in PARITIES] for by, bx in BLOCKS]
FAR = [[device_of(2 * by + qy, 2 * bx + qx) for by, bx in BLOCKS] for qy, qx in PARITIES]


def odd_pair(y, x, along_y):
    if along_y:
        return device_of(y + 2 * (y % 2) - 1, x)
    return device_of(y, x + 2 * (x % 2) - 1)


def swap(value, turn):
    slabs = lax.axis_size("gz")
    moves = [
        (device_of(y, x) * slabs + z, odd_pair(y, x, (z + turn) % 2) * slabs + z)
        for y in range(NY)
        for x in range(NX)
        for z in range(slabs)
    ]
    return lax.ppermute(value, ("xy", "gz"), moves)


def exchange(value, groups):
    return lax.all_to_all(
        value, "xy", split_axis=0, concat_axis=0, axis_index_groups=groups, tiled=True
    )


def split3(value):
    high = value.astype(jnp.bfloat16)
    rest = value - high.astype(jnp.float32)
    mid = rest.astype(jnp.bfloat16)
    low = (rest - mid.astype(jnp.float32)).astype(jnp.bfloat16)
    return [high, mid, low]


def with_ones(value):
    ones = jnp.ones((16, value.shape[1]), jnp.bfloat16)
    return jnp.concatenate(split3(value) + [ones], axis=0)


def place(owner, me):
    y, x = owner // NX, owner % NX
    my_y, my_x, core = me[0] // NX, me[0] % NX, me[1]
    other_x, other_y = (x + my_x) % 2, (y + my_y) % 2
    quad = (y % 2) * 2 + x % 2
    slot = (y // 2) * BX + x // 2
    return quad, slot, other_x + core * (other_y - other_x), other_y + core * (other_x - other_y)


def join3(product, rows):
    return product[2 * rows : 3 * rows] + product[rows : 2 * rows] + product[:rows]


def fetch_all(pairs, sems):
    copies = [pltpu.make_async_copy(src, dst, sems.at[i]) for i, (src, dst) in enumerate(pairs)]
    for copy in copies:
        copy.start()
    return copies


def pinned(value, space):
    return pltpu.with_memory_space_constraint(value, space)


ANY = pl.BlockSpec(memory_space=pl.ANY)
SMEM = pl.BlockSpec(memory_space=pltpu.SMEM)
VMEM = pl.BlockSpec(memory_space=pltpu.VMEM)
PARAMS = pltpu.CompilerParams(vmem_limit_bytes=VMEM_LIMIT)


def small_scratch(lists, owners, starts):
    return [pltpu.SMEM(a.shape, jnp.int32) for a in (lists, owners, starts)]


def slot_rows(slot, rows):
    return pl.ds(pl.multiple_of(slot * rows, 8), rows)


def fetch_mats(mats_hbm, mats, sems):
    return fetch_all(
        [
            (mats_hbm.at[0, pl.ds(k, MATS_AT_ONCE)], mats.at[pl.ds(k, MATS_AT_ONCE)])
            for k in range(0, mats.shape[0], MATS_AT_ONCE)
        ],
        sems,
    )


def wait_mats(copies, k):
    if k % MATS_AT_ONCE == 0:
        copies[k // MATS_AT_ONCE].wait()


def mats_scratch(mats, others):
    count = mats.shape[1]
    return [
        pltpu.VMEM(mats.shape[1:], jnp.bfloat16),
        pltpu.SemaphoreType.DMA((others,)),
        pltpu.SemaphoreType.DMA((count // MATS_AT_ONCE,)),
    ]


def project_kernel(
    me_ref, lists_hbm, owners_hbm, starts_hbm, vol_hbm, mats_hbm,
    a_ref, keep_ref, send_ref, lists, owners, starts, wide, part, mats, sems, mat_sems,
):
    rows, cols = vol_hbm.shape
    count = mats.shape[0]
    copies = fetch_all(
        [
            (lists_hbm, lists),
            (owners_hbm, owners),
            (starts_hbm, starts),
            (vol_hbm, wide.at[:, pl.ds(0, cols)]),
        ],
        sems,
    )
    mat_copies = fetch_mats(mats_hbm, mats, mat_sems)
    wide[:, cols:] = jnp.zeros((rows, LANES), jnp.float32)
    for ref in (a_ref, part):
        ref[...] = jnp.zeros(ref.shape, jnp.float32)
    for copy in copies:
        copy.wait()
    me = me_ref[0], me_ref[1]
    for k in range(count):
        start = starts[0, k]
        quad, slot, across0, across1 = place(owners[0, lists[k, me[0]]], me)
        base = pl.multiple_of((start // LANES) * LANES, LANES)
        window = wide[:, pl.ds(base, W + LANES)]
        window = pltpu.roll(window, (W + LANES) - start % LANES, 1)[:, :W]
        wait_mats(mat_copies, k)
        product = jnp.dot(with_ones(window), mats[k], preferred_element_type=jnp.float32)
        value = join3(product, rows)
        a_ref[quad, slot_rows(slot, ROWS_A), :] = value[:ROWS_A]
        a_ref[quad, pl.ds(SLOTS * ROWS_A + slot, 1), :] = product[3 * rows : 3 * rows + 1]
        part[across0, across1, slot_rows(slot, ROWS_B), :] = value[ROWS_A:]
    keep_ref[...] = part[0]
    send_ref[...] = part[1]


def project(me, lists, owners, starts, volume, mats):
    rows, cols = volume.shape
    operands = [pinned(a, pltpu.HBM) for a in (lists, owners, starts, volume, mats)]
    half = pltpu.VMEM((2, SLOTS * ROWS_B, W), jnp.float32)
    return pl.pallas_call(
        project_kernel,
        out_shape=[jax.ShapeDtypeStruct((QUAD, SLOTS * ROWS_A + SLOTS, W), jnp.float32)]
        + [half] * 2,
        in_specs=[SMEM] + [ANY] * 5,
        out_specs=[VMEM] * 3,
        scratch_shapes=small_scratch(lists, owners, starts)
        + [pltpu.VMEM((rows, cols + LANES), jnp.float32)]
        + [pltpu.VMEM((2, 2, SLOTS * ROWS_B, W), jnp.float32)]
        + mats_scratch(mats, 4),
        compiler_params=PARAMS,
    )(me, *operands)


def turn_kernel(keep, came, own, send):
    own[...] = keep[0] + came[0]
    send[...] = keep[1] + came[1]


def turn(keep, came):
    return pl.pallas_call(
        turn_kernel,
        out_shape=[pltpu.VMEM((SLOTS * ROWS_B, W), jnp.float32)] * 2,
        in_specs=[VMEM] * 2,
        out_specs=[VMEM] * 2,
        compiler_params=PARAMS,
    )(pinned(keep, pltpu.VMEM), pinned(came, pltpu.VMEM))


def gather_kernel(a_ref, own, came, vol_hbm, out_ref, first_ref, last_ref, ends, sems):
    height = vol_hbm.shape[0]
    copies = fetch_all(
        [
            (vol_hbm.at[pl.ds(0, 8)], ends.at[0]),
            (vol_hbm.at[pl.ds(height - 8, 8)], ends.at[1]),
        ],
        sems,
    )
    total = a_ref[0]
    for i in range(1, QUAD):
        total = total + a_ref[i]
    total_b = own[...] + came[...]
    for slot in range(SLOTS):
        out_ref[slot, :ROWS_A] = total[slot * ROWS_A : (slot + 1) * ROWS_A]
        rows = ROWS_A + ROWS_B
        out_ref[slot, ROWS_A:rows] = total_b[slot * ROWS_B : (slot + 1) * ROWS_B]
        at = SLOTS * ROWS_A + slot
        out_ref[slot, rows:] = jnp.broadcast_to(total[at : at + 1], (8, W))
    for copy in copies:
        copy.wait()
    first_ref[...] = ends[0, :1]
    last_ref[...] = ends[1, 7:]


def gather_near(arrived, own, came, volume):
    rows, cols = volume.shape
    face = jax.ShapeDtypeStruct((1, cols), jnp.float32)
    return pl.pallas_call(
        gather_kernel,
        out_shape=[pltpu.VMEM((SLOTS, rows + 8, W), jnp.float32), face, face],
        in_specs=[VMEM] * 3 + [ANY],
        out_specs=[VMEM] * 3,
        scratch_shapes=[pltpu.VMEM((2, 8, cols), jnp.float32), pltpu.SemaphoreType.DMA((2,))],
        compiler_params=PARAMS,
    )(arrived, own, came, pinned(volume, pltpu.HBM))


def spread_kernel(column_ref, after_ref, a_ref, b_ref):
    for slot in range(SLOTS):
        for i in range(QUAD):
            a_ref[i, slot * ROWS_A : (slot + 1) * ROWS_A] = column_ref[slot, :ROWS_A]
        b_ref[slot * ROWS_B : (slot + 1) * ROWS_B] = column_ref[slot, ROWS_A:]


def spread_near(column, after):
    part = pltpu.VMEM((SLOTS * ROWS_B, W), jnp.float32)
    return pl.pallas_call(
        spread_kernel,
        out_shape=[jax.ShapeDtypeStruct((QUAD, SLOTS * ROWS_A, W), jnp.float32), part],
        in_specs=[VMEM, ANY],
        out_specs=[VMEM] * 2,
        compiler_params=PARAMS,
    )(column, after)


def stack_kernel(own, came, pair):
    pair[0] = own[...]
    pair[1] = came[...]


def stack_pair(own, came):
    return pl.pallas_call(
        stack_kernel,
        out_shape=pltpu.VMEM((2, SLOTS * ROWS_B, W), jnp.float32),
        in_specs=[VMEM] * 2,
        out_specs=VMEM,
        compiler_params=PARAMS,
    )(pinned(own, pltpu.VMEM), pinned(came, pltpu.VMEM))


def back_kernel(
    me_ref, lists_hbm, owners_hbm, starts_hbm, mats_hbm,
    base_ref, a_ref, own, came, out_ref, lists, owners, starts, total, part, mats, sems, mat_sems,
):
    rows, cols = base_ref.shape
    count = mats.shape[0]
    copies = fetch_all([(lists_hbm, lists), (owners_hbm, owners), (starts_hbm, starts)], sems)
    mat_copies = fetch_mats(mats_hbm, mats, mat_sems)
    total[...] = jnp.zeros(total.shape, jnp.float32)
    part[0] = own[...]
    part[1] = came[...]
    for copy in copies:
        copy.wait()
    me = me_ref[0], me_ref[1]
    for k in range(count):
        start = starts[0, k]
        quad, slot, across0, across1 = place(owners[0, lists[k, me[0]]], me)
        base = pl.multiple_of((start // LANES) * LANES, LANES)
        needed = jnp.concatenate(
            [
                a_ref[quad, slot_rows(slot, ROWS_A), :],
                part[across0, across1, slot_rows(slot, ROWS_B), :],
            ],
            axis=0,
        )
        wait_mats(mat_copies, k)
        product = lax.dot_general(
            with_ones(needed),
            mats[k],
            (((1,), (1,)), ((), ())),
            preferred_element_type=jnp.float32,
        )
        value = jnp.concatenate([join3(product, rows), product[3 * rows : 3 * rows + 8]], axis=0)
        value = jnp.concatenate([value, jnp.zeros((rows + 8, LANES), jnp.float32)], axis=1)
        total[:, pl.ds(base, W + LANES)] += pltpu.roll(value, start % LANES, 1)
    column = jnp.maximum(total[rows : rows + 1, :cols], 1.0)
    out_ref[...] = base_ref[...] + relax * (total[:rows, :cols] / column)


def back_project(me, lists, owners, starts, base, mats, *parts):
    rows, cols = base.shape
    operands = [pinned(a, pltpu.HBM) for a in (lists, owners, starts, mats)]
    operands += [pinned(a, pltpu.VMEM) for a in (base,) + parts]
    return pl.pallas_call(
        back_kernel,
        out_shape=jax.ShapeDtypeStruct((rows, cols), jnp.float32),
        in_specs=[SMEM] + [ANY] * 4 + [VMEM] * 4,
        out_specs=VMEM,
        scratch_shapes=small_scratch(lists, owners, starts)
        + [pltpu.VMEM((rows + 8, cols + LANES), jnp.float32)]
        + [pltpu.VMEM((2, 2, SLOTS * ROWS_B, W), jnp.float32)]
        + mats_scratch(mats, 3),
        compiler_params=PARAMS,
    )(me, *operands)


def with_faces(volume, first, last):
    count = lax.axis_size("gz")
    up = [(i, i + 1) for i in range(count - 1)]
    down = [(i + 1, i) for i in range(count - 1)]
    return jnp.concatenate(
        [lax.ppermute(last, "gz", up), volume, lax.ppermute(first, "gz", down)], axis=0
    )


def total_variation(padded):
    diffs = padded[1:] - padded[:-1]
    slopes = diffs / jnp.sqrt(diffs * diffs + smooth_sq)
    return slopes[:-1] - slopes[1:]


def per_device(volume, sinogram, ray_mats, offsets, ray_lists, owner_map):
    rows = volume.shape[0]
    me = jnp.stack([lax.axis_index("xy"), lax.axis_index("gz") % 2]).astype(jnp.int32)
    plan = (me, ray_lists.T, owner_map.reshape(1, -1), offsets)
    a, keep, send = project(*plan, volume, ray_mats)
    own, send = turn(keep, swap(send, 0))
    outgoing, first, last = gather_near(exchange(a, NEAR), own, swap(send, 1), volume)
    arrived = jnp.sum(exchange(outgoing, FAR), axis=0)
    base = volume - tv_weight * total_variation(with_faces(volume, first, last))
    weighted = (sinogram - arrived[:rows]) / arrived[rows : rows + 1]
    column = exchange(jnp.broadcast_to(weighted[None], (SLOTS, rows, W)), FAR)
    a, own = spread_near(column, base)
    pair = stack_pair(own, swap(own, 1))
    got = (exchange(a, NEAR), pair, swap(pair, 0))
    new_volume = back_project(*plan, base, ray_mats, *got)
    return (new_volume, weighted)


def solution(mesh):
    in_specs = (P("gz", "xy"), P("gz", "xy"), P("xy", None, None, None), P("xy", None), P(), P())
    out_specs = (P("gz", "xy"), P("gz", "xy"))
    return jax.shard_map(
        per_device, mesh=mesh, in_specs=in_specs, out_specs=out_specs, check_vma=False
    )
```

```python
import functools

import jax
import jax.numpy as jnp
from jax import lax
from jax.experimental import pallas as pl
from jax.experimental.pallas import tpu as pltpu
from jax.sharding import PartitionSpec as P

relax = 1.0
tv_weight = 0.2
smooth_sq = 0.01

NX, NY = 4, 8
BX, BY = NX // 2, NY // 2
QUAD, SLOTS = 4, BX * BY
W = 256
LANES = 128
VMEM_LIMIT = 32 * 1024 * 1024


def device_of(y, x):
    return (y % NY) * NX + x % NX


PLACES = [(qy, qx) for qy in range(2) for qx in range(2)]
BLOCKS = [(by, bx) for by in range(BY) for bx in range(BX)]


def exchange(value, near):
    slabs = lax.axis_size("gz")

    def member(slab, block, place):
        core = slab % 2
        y, x = 2 * block[0] + place[0] + core, 2 * block[1] + place[1] + core
        return device_of(y, x) * slabs + slab

    groups = []
    for slab in range(slabs):
        if near:
            groups += [[member(slab, block, place) for place in PLACES] for block in BLOCKS]
        else:
            groups += [[member(slab, block, place) for block in BLOCKS] for place in PLACES]
    return lax.all_to_all(
        value, ("xy", "gz"), split_axis=0, concat_axis=0, axis_index_groups=groups, tiled=True
    )


def split3(value):
    high = value.astype(jnp.bfloat16)
    rest = value - high.astype(jnp.float32)
    mid = rest.astype(jnp.bfloat16)
    low = (rest - mid.astype(jnp.float32)).astype(jnp.bfloat16)
    return [high, mid, low]


def with_ones(value):
    ones = jnp.ones((16, value.shape[1]), jnp.bfloat16)
    return jnp.concatenate(split3(value) + [ones], axis=0)


def near_far(owner, core):
    y, x = (owner // NX + NY - core) % NY, (owner % NX + NX - core) % NX
    return (y % 2) * 2 + x % 2, (y // 2) * BX + x // 2


def join3(product, rows):
    return product[2 * rows : 3 * rows] + product[rows : 2 * rows] + product[:rows]


def fetch_all(pairs, sems):
    copies = [pltpu.make_async_copy(src, dst, sems.at[i]) for i, (src, dst) in enumerate(pairs)]
    for copy in copies:
        copy.start()
    return copies


def pinned(value, space):
    return pltpu.with_memory_space_constraint(value, space)


ANY = pl.BlockSpec(memory_space=pl.ANY)
SMEM = pl.BlockSpec(memory_space=pltpu.SMEM)
VMEM = pl.BlockSpec(memory_space=pltpu.VMEM)
PARAMS = pltpu.CompilerParams(vmem_limit_bytes=VMEM_LIMIT)


def small_scratch(lists, owners, starts):
    return [pltpu.SMEM(a.shape, jnp.int32) for a in (lists, owners, starts)]


def project_kernel(
    me_ref, lists_hbm, owners_hbm, starts_hbm, vol_hbm, mats_hbm, out_ref, mats_ref,
    lists, owners, starts, wide, sems,
):
    rows, cols = vol_hbm.shape
    count = mats_ref.shape[0]
    copies = fetch_all(
        [
            (lists_hbm, lists),
            (owners_hbm, owners),
            (starts_hbm, starts),
            (vol_hbm, wide.at[:, pl.ds(0, cols)]),
            (mats_hbm.at[0], mats_ref),
        ],
        sems,
    )
    wide[:, cols:] = jnp.zeros((rows, LANES), jnp.float32)
    out_ref[...] = jnp.zeros(out_ref.shape, jnp.float32)
    for copy in copies:
        copy.wait()
    me, core = me_ref[0], me_ref[1]
    for k in range(count):
        start = starts[0, k]
        near, far = near_far(owners[0, lists[k, me]], core)
        base = pl.multiple_of((start // LANES) * LANES, LANES)
        window = wide[:, pl.ds(base, W + LANES)]
        window = pltpu.roll(window, (W + LANES) - start % LANES, 1)[:, :W]
        product = jnp.dot(with_ones(window), mats_ref[k], preferred_element_type=jnp.float32)
        out_ref[near, pl.ds(pl.multiple_of(far * rows, 8), rows), :] = join3(product, rows)
        out_ref[near, pl.ds(SLOTS * rows + far, 1), :] = product[3 * rows : 3 * rows + 1]


def project(me, lists, owners, starts, volume, mats):
    rows, cols = volume.shape
    operands = [pinned(a, pltpu.HBM) for a in (lists, owners, starts, volume, mats)]
    return pl.pallas_call(
        project_kernel,
        out_shape=[
            pltpu.VMEM((QUAD, SLOTS * rows + 8, W), jnp.float32),
            pltpu.VMEM(mats.shape[1:], jnp.bfloat16),
        ],
        in_specs=[SMEM] + [ANY] * 5,
        out_specs=[VMEM, VMEM],
        scratch_shapes=small_scratch(lists, owners, starts)
        + [pltpu.VMEM((rows, cols + LANES), jnp.float32), pltpu.SemaphoreType.DMA((5,))],
        compiler_params=PARAMS,
    )(me, *operands)


def gather_kernel(rows, in_ref, vol_hbm, out_ref, first_ref, last_ref, ends, sems):
    height = vol_hbm.shape[0]
    copies = fetch_all(
        [
            (vol_hbm.at[pl.ds(0, 8)], ends.at[0]),
            (vol_hbm.at[pl.ds(height - 8, 8)], ends.at[1]),
        ],
        sems,
    )
    total = in_ref[0]
    for i in range(1, QUAD):
        total = total + in_ref[i]
    for far in range(SLOTS):
        out_ref[far, :rows] = total[far * rows : (far + 1) * rows]
        out_ref[far, rows:] = jnp.broadcast_to(
            total[SLOTS * rows + far : SLOTS * rows + far + 1], (8, W)
        )
    for copy in copies:
        copy.wait()
    first_ref[...] = ends[0, :1]
    last_ref[...] = ends[1, 7:]


def gather_near(arrived, volume):
    rows, cols = volume.shape
    face = jax.ShapeDtypeStruct((1, cols), jnp.float32)
    return pl.pallas_call(
        functools.partial(gather_kernel, rows),
        out_shape=[jax.ShapeDtypeStruct((SLOTS, rows + 8, W), jnp.float32), face, face],
        in_specs=[VMEM, ANY],
        out_specs=[VMEM] * 3,
        scratch_shapes=[pltpu.VMEM((2, 8, cols), jnp.float32), pltpu.SemaphoreType.DMA((2,))],
        compiler_params=PARAMS,
    )(pinned(arrived, pltpu.VMEM), pinned(volume, pltpu.HBM))


def spread_kernel(column_ref, after_ref, out_ref):
    for i in range(QUAD):
        out_ref[i] = column_ref[...]


def spread_near(column, after):
    return pl.pallas_call(
        spread_kernel,
        out_shape=pltpu.VMEM((QUAD,) + column.shape, jnp.float32),
        in_specs=[VMEM, ANY],
        out_specs=VMEM,
        compiler_params=PARAMS,
    )(column, after)


def back_kernel(
    me_ref, lists_hbm, owners_hbm, starts_hbm, base_ref, mats_ref, got_ref, out_ref,
    lists, owners, starts, total, sems,
):
    rows, cols = base_ref.shape
    count = mats_ref.shape[0]
    copies = fetch_all([(lists_hbm, lists), (owners_hbm, owners), (starts_hbm, starts)], sems)
    total[...] = jnp.zeros(total.shape, jnp.float32)
    for copy in copies:
        copy.wait()
    me, core = me_ref[0], me_ref[1]
    for k in range(count):
        start = starts[0, k]
        near, far = near_far(owners[0, lists[k, me]], core)
        base = pl.multiple_of((start // LANES) * LANES, LANES)
        product = lax.dot_general(
            with_ones(got_ref[near, far]),
            mats_ref[k],
            (((1,), (1,)), ((), ())),
            preferred_element_type=jnp.float32,
        )
        value = jnp.concatenate([join3(product, rows), product[3 * rows : 3 * rows + 8]], axis=0)
        value = jnp.concatenate([value, jnp.zeros((rows + 8, LANES), jnp.float32)], axis=1)
        total[:, pl.ds(base, W + LANES)] += pltpu.roll(value, start % LANES, 1)
    column = jnp.maximum(total[rows : rows + 1, :cols], 1.0)
    out_ref[...] = base_ref[...] + relax * (total[:rows, :cols] / column)


def back_project(me, lists, owners, starts, base, mats, got):
    rows, cols = base.shape
    operands = [pinned(a, pltpu.HBM) for a in (lists, owners, starts)]
    operands += [pinned(a, pltpu.VMEM) for a in (base, mats, got)]
    return pl.pallas_call(
        back_kernel,
        out_shape=jax.ShapeDtypeStruct((rows, cols), jnp.float32),
        in_specs=[SMEM] + [ANY] * 3 + [VMEM] * 3,
        out_specs=VMEM,
        scratch_shapes=small_scratch(lists, owners, starts)
        + [pltpu.VMEM((rows + 8, cols + LANES), jnp.float32), pltpu.SemaphoreType.DMA((3,))],
        compiler_params=PARAMS,
    )(me, *operands)


def with_faces(volume, first, last):
    count = lax.axis_size("gz")
    up = [(i, i + 1) for i in range(count - 1)]
    down = [(i + 1, i) for i in range(count - 1)]
    return jnp.concatenate(
        [lax.ppermute(last, "gz", up), volume, lax.ppermute(first, "gz", down)], axis=0
    )


def total_variation(padded):
    diffs = padded[1:] - padded[:-1]
    slopes = diffs / jnp.sqrt(diffs * diffs + smooth_sq)
    return slopes[:-1] - slopes[1:]


def per_device(volume, sinogram, ray_mats, offsets, ray_lists, owner_map):
    rows = volume.shape[0]
    me = jnp.stack([lax.axis_index("xy"), lax.axis_index("gz") % 2]).astype(jnp.int32)
    plan = (me, ray_lists.T, owner_map.reshape(1, -1), offsets)
    outgoing, mats = project(*plan, volume, ray_mats)
    outgoing, first, last = gather_near(exchange(outgoing, True), volume)
    arrived = jnp.sum(exchange(outgoing, False), axis=0)
    base = volume - tv_weight * total_variation(with_faces(volume, first, last))
    weighted = (sinogram - arrived[:rows]) / arrived[rows : rows + 1]
    column = exchange(jnp.broadcast_to(weighted[None], (SLOTS, rows, W)), False)
    got = exchange(spread_near(column, base), True)
    new_volume = back_project(*plan, base, mats, got)
    return (new_volume, weighted)


def solution(mesh):
    in_specs = (P("gz", "xy"), P("gz", "xy"), P("xy", None, None, None), P("xy", None), P(), P())
    out_specs = (P("gz", "xy"), P("gz", "xy"))
    return jax.shard_map(
        per_device, mesh=mesh, in_specs=in_specs, out_specs=out_specs, check_vma=False
    )
```

```python
import functools

import jax
import jax.numpy as jnp
from jax import lax
from jax.experimental import pallas as pl
from jax.experimental.pallas import tpu as pltpu
from jax.sharding import PartitionSpec as P

relax = 1.0
tv_weight = 0.2
smooth_sq = 0.01

NX, NY = 4, 8
BX, BY = NX // 2, NY // 2
QUAD, SLOTS, FAR = 4, 8, 2
W = 256
LANES = 128
VMEM_LIMIT = 32 * 1024 * 1024


def device_of(y, x):
    return (y % NY) * NX + x % NX


PLACES = [(qy, qx) for qy in range(2) for qx in range(2)]
BLOCKS = [(by, bx) for by in range(BY) for bx in range(BX)]


def exchange(value, level):
    slabs = lax.axis_size("gz")

    def member(slab, block, place):
        shift = slab % 2 + level - 1
        y, x = 2 * block[0] + place[0] + shift, 2 * block[1] + place[1] + shift
        return device_of(y, x) * slabs + slab

    groups = [
        [member(slab, block, place) for place in PLACES] for slab in range(slabs) for block in BLOCKS
    ]
    return lax.all_to_all(
        value, ("xy", "gz"), split_axis=0, concat_axis=0, axis_index_groups=groups, tiled=True
    )


def swap_far(value):
    moves = [(device_of(y, x), device_of(y + BY, x)) for y in range(NY) for x in range(NX)]
    return lax.ppermute(value, "xy", moves)


def split3(value):
    high = value.astype(jnp.bfloat16)
    rest = value - high.astype(jnp.float32)
    mid = rest.astype(jnp.bfloat16)
    low = (rest - mid.astype(jnp.float32)).astype(jnp.bfloat16)
    return [high, mid, low]


def with_ones(value):
    ones = jnp.ones((16, value.shape[1]), jnp.bfloat16)
    return jnp.concatenate(split3(value) + [ones], axis=0)


def shifted(device, core):
    return (device // NX + NY - core) % NY, (device % NX + NX - core) % NX


def near_far(owner, me, core):
    (y, x), (my_y, my_x) = shifted(owner, core), shifted(me, core)
    near_y = ((y + 1) // 2 + my_y // 2) % 2
    near_x = ((x + 1) // 2 + my_x // 2) % 2
    place = (y + 1) % 2 * 2 + (x + 1) % 2
    return near_y * 2 + near_x, place * FAR + y // BY


def join3(product, rows):
    return product[2 * rows : 3 * rows] + product[rows : 2 * rows] + product[:rows]


def fetch_all(pairs, sems):
    copies = [pltpu.make_async_copy(src, dst, sems.at[i]) for i, (src, dst) in enumerate(pairs)]
    for copy in copies:
        copy.start()
    return copies


def pinned(value, space):
    return pltpu.with_memory_space_constraint(value, space)


ANY = pl.BlockSpec(memory_space=pl.ANY)
SMEM = pl.BlockSpec(memory_space=pltpu.SMEM)
VMEM = pl.BlockSpec(memory_space=pltpu.VMEM)
PARAMS = pltpu.CompilerParams(vmem_limit_bytes=VMEM_LIMIT)


def small_scratch(lists, owners, starts):
    return [pltpu.SMEM(a.shape, jnp.int32) for a in (lists, owners, starts)]


def project_kernel(
    me_ref, lists_hbm, owners_hbm, starts_hbm, vol_hbm, mats_hbm,
    out_ref, mats_ref, first_ref, last_ref, lists, owners, starts, wide, sems,
):
    rows, cols = vol_hbm.shape
    count = mats_ref.shape[0]
    copies = fetch_all(
        [
            (lists_hbm, lists),
            (owners_hbm, owners),
            (starts_hbm, starts),
            (vol_hbm, wide.at[:, pl.ds(0, cols)]),
            (mats_hbm.at[0], mats_ref),
        ],
        sems,
    )
    wide[:, cols:] = jnp.zeros((rows, LANES), jnp.float32)
    out_ref[...] = jnp.zeros(out_ref.shape, jnp.float32)
    for copy in copies:
        copy.wait()
    first_ref[...] = wide[:1, :cols]
    last_ref[...] = wide[rows - 1 :, :cols]
    me, core = me_ref[0], me_ref[1]
    for k in range(count):
        start = starts[0, k]
        near, far = near_far(owners[0, lists[k, me]], me, core)
        base = pl.multiple_of((start // LANES) * LANES, LANES)
        window = wide[:, pl.ds(base, W + LANES)]
        window = pltpu.roll(window, (W + LANES) - start % LANES, 1)[:, :W]
        product = jnp.dot(with_ones(window), mats_ref[k], preferred_element_type=jnp.float32)
        out_ref[near, pl.ds(pl.multiple_of(far * rows, 8), rows), :] = join3(product, rows)
        out_ref[near, pl.ds(SLOTS * rows + far, 1), :] = product[3 * rows : 3 * rows + 1]


def project(me, lists, owners, starts, volume, mats):
    rows, cols = volume.shape
    operands = [pinned(a, pltpu.HBM) for a in (lists, owners, starts, volume, mats)]
    return pl.pallas_call(
        project_kernel,
        out_shape=[
            pltpu.VMEM((QUAD, SLOTS * rows + 8, W), jnp.float32),
            pltpu.VMEM(mats.shape[1:], jnp.bfloat16),
            pltpu.VMEM((1, cols), jnp.float32),
            pltpu.VMEM((1, cols), jnp.float32),
        ],
        in_specs=[SMEM] + [ANY] * 5,
        out_specs=[VMEM] * 4,
        scratch_shapes=small_scratch(lists, owners, starts)
        + [pltpu.VMEM((rows, cols + LANES), jnp.float32), pltpu.SemaphoreType.DMA((5,))],
        compiler_params=PARAMS,
    )(me, *operands)


def sum_quad(ref):
    return ref[0] + ref[1] + ref[2] + ref[3]


def gather_near_kernel(rows, in_ref, first_in, last_in, out_ref, first_ref, last_ref):
    total = sum_quad(in_ref)
    for place in range(QUAD):
        at = place * FAR
        out_ref[place, : FAR * rows] = total[at * rows : (at + FAR) * rows]
        sums = total[SLOTS * rows + at : SLOTS * rows + at + FAR]
        out_ref[place, FAR * rows : FAR * rows + FAR] = sums
        out_ref[place, FAR * rows + FAR :] = jnp.zeros((8 - FAR, W), jnp.float32)
    first_ref[...] = first_in[...]
    last_ref[...] = last_in[...]


def gather_near(arrived, first, last):
    rows = (arrived.shape[1] - 8) // SLOTS
    face = jax.ShapeDtypeStruct(first.shape, jnp.float32)
    return pl.pallas_call(
        functools.partial(gather_near_kernel, rows),
        out_shape=[pltpu.VMEM((QUAD, FAR * rows + 8, W), jnp.float32), face, face],
        in_specs=[VMEM] * 3,
        out_specs=[VMEM] * 3,
        compiler_params=PARAMS,
    )(*(pinned(a, pltpu.VMEM) for a in (arrived, first, last)))


def gather_far_kernel(rows, me_ref, in_ref, keep_ref, send_ref, total):
    half = shifted(me_ref[0], me_ref[1])[0] // BY
    total[...] = sum_quad(in_ref)
    for ref, side in ((keep_ref, half), (send_ref, 1 - half)):
        ref[:rows] = total[pl.ds(pl.multiple_of(side * rows, 8), rows), :]
        ref[rows:] = jnp.broadcast_to(total[pl.ds(FAR * rows + side, 1), :], (8, W))


def gather_far(me, arrived):
    rows = (arrived.shape[1] - 8) // FAR
    return pl.pallas_call(
        functools.partial(gather_far_kernel, rows),
        out_shape=[pltpu.VMEM((rows + 8, W), jnp.float32)] * 2,
        in_specs=[SMEM, VMEM],
        out_specs=[VMEM] * 2,
        scratch_shapes=[pltpu.VMEM(arrived.shape[1:], jnp.float32)],
        compiler_params=PARAMS,
    )(me, pinned(arrived, pltpu.VMEM))


def spread_far_kernel(me_ref, own_ref, came_ref, out_ref):
    half = shifted(me_ref[0], me_ref[1])[0] // BY
    rows = own_ref.shape[0]
    for place in range(QUAD):
        out_ref[place, pl.ds(pl.multiple_of(half * rows, 8), rows), :] = own_ref[...]
        out_ref[place, pl.ds(pl.multiple_of((1 - half) * rows, 8), rows), :] = came_ref[...]


def spread_far(me, own, came):
    rows = own.shape[0]
    return pl.pallas_call(
        spread_far_kernel,
        out_shape=jax.ShapeDtypeStruct((QUAD, FAR * rows, W), jnp.float32),
        in_specs=[SMEM, VMEM, VMEM],
        out_specs=VMEM,
        compiler_params=PARAMS,
    )(me, own, came)


def spread_near_kernel(column_ref, after_ref, out_ref):
    for place in range(QUAD):
        out_ref[place] = column_ref[...]


def spread_near(column, after):
    return pl.pallas_call(
        spread_near_kernel,
        out_shape=pltpu.VMEM((QUAD,) + column.shape, jnp.float32),
        in_specs=[VMEM, ANY],
        out_specs=VMEM,
        compiler_params=PARAMS,
    )(column, after)


def back_kernel(
    me_ref, lists_hbm, owners_hbm, starts_hbm, base_ref, mats_ref, got_ref, out_ref,
    lists, owners, starts, total, sems,
):
    rows, cols = base_ref.shape
    count = mats_ref.shape[0]
    copies = fetch_all([(lists_hbm, lists), (owners_hbm, owners), (starts_hbm, starts)], sems)
    total[...] = jnp.zeros(total.shape, jnp.float32)
    for copy in copies:
        copy.wait()
    me, core = me_ref[0], me_ref[1]
    for k in range(count):
        start = starts[0, k]
        near, far = near_far(owners[0, lists[k, me]], me, core)
        base = pl.multiple_of((start // LANES) * LANES, LANES)
        product = lax.dot_general(
            with_ones(got_ref[near, far]),
            mats_ref[k],
            (((1,), (1,)), ((), ())),
            preferred_element_type=jnp.float32,
        )
        value = jnp.concatenate([join3(product, rows), product[3 * rows : 3 * rows + 8]], axis=0)
        value = jnp.concatenate([value, jnp.zeros((rows + 8, LANES), jnp.float32)], axis=1)
        total[:, pl.ds(base, W + LANES)] += pltpu.roll(value, start % LANES, 1)
    column = jnp.maximum(total[rows : rows + 1, :cols], 1.0)
    out_ref[...] = base_ref[...] + relax * (total[:rows, :cols] / column)


def back_project(me, lists, owners, starts, base, mats, got):
    rows, cols = base.shape
    operands = [pinned(a, pltpu.HBM) for a in (lists, owners, starts)]
    operands += [pinned(a, pltpu.VMEM) for a in (base, mats, got)]
    return pl.pallas_call(
        back_kernel,
        out_shape=jax.ShapeDtypeStruct((rows, cols), jnp.float32),
        in_specs=[SMEM] + [ANY] * 3 + [VMEM] * 3,
        out_specs=VMEM,
        scratch_shapes=small_scratch(lists, owners, starts)
        + [pltpu.VMEM((rows + 8, cols + LANES), jnp.float32), pltpu.SemaphoreType.DMA((3,))],
        compiler_params=PARAMS,
    )(me, *operands)


def with_faces(volume, first, last):
    count = lax.axis_size("gz")
    up = [(i, i + 1) for i in range(count - 1)]
    down = [(i + 1, i) for i in range(count - 1)]
    return jnp.concatenate(
        [lax.ppermute(last, "gz", up), volume, lax.ppermute(first, "gz", down)], axis=0
    )


def total_variation(padded):
    diffs = padded[1:] - padded[:-1]
    slopes = diffs / jnp.sqrt(diffs * diffs + smooth_sq)
    return slopes[:-1] - slopes[1:]


def per_device(volume, sinogram, ray_mats, offsets, ray_lists, owner_map):
    rows = volume.shape[0]
    core = lax.axis_index("gz") % 2
    device = lax.axis_index("xy")
    me = jnp.stack([device, core]).astype(jnp.int32)
    plan = (me, ray_lists.T, owner_map.reshape(1, -1), offsets)
    outgoing, mats, first, last = project(*plan, volume, ray_mats)
    outgoing, first, last = gather_near(exchange(outgoing, 1), first, last)
    keep, send = gather_far(me, exchange(outgoing, 2))
    total = keep + swap_far(send)
    base = volume - tv_weight * total_variation(with_faces(volume, first, last))
    weighted = (sinogram - total[:rows]) / total[rows : rows + 1]
    column = exchange(spread_far(me, weighted, swap_far(weighted)), 2)
    column = column.reshape(SLOTS, rows, W)
    got = exchange(spread_near(column, base), 1)
    new_volume = back_project(*plan, base, mats, got)
    return (new_volume, weighted)


def solution(mesh):
    in_specs = (P("gz", "xy"), P("gz", "xy"), P("xy", None, None, None), P("xy", None), P(), P())
    out_specs = (P("gz", "xy"), P("gz", "xy"))
    return jax.shard_map(
        per_device, mesh=mesh, in_specs=in_specs, out_specs=out_specs, check_vma=False
    )
```

```python
import functools

import jax
import jax.numpy as jnp
from jax import lax
from jax.experimental import pallas as pl
from jax.experimental.pallas import tpu as pltpu
from jax.sharding import PartitionSpec as P

relax = 1.0
tv_weight = 0.2
smooth_sq = 0.01

NX, NY = 4, 8
BX, BY = NX // 2, NY // 2
QUAD, SLOTS, FAR = 4, 8, 2
MATS_AT_ONCE = 4
W = 256
LANES = 128
VMEM_LIMIT = 32 * 1024 * 1024


def device_of(y, x):
    return (y % NY) * NX + x % NX


PLACES = [(qy, qx) for qy in range(2) for qx in range(2)]
BLOCKS = [(by, bx) for by in range(BY) for bx in range(BX)]


def exchange(value, level):
    slabs = lax.axis_size("gz")

    def member(slab, block, place):
        shift = slab % 2 + level - 1
        y, x = 2 * block[0] + place[0] + shift, 2 * block[1] + place[1] + shift
        return device_of(y, x) * slabs + slab

    groups = [
        [member(slab, block, place) for place in PLACES] for slab in range(slabs) for block in BLOCKS
    ]
    return lax.all_to_all(
        value, ("xy", "gz"), split_axis=0, concat_axis=0, axis_index_groups=groups, tiled=True
    )


def swap_far(value):
    moves = [(device_of(y, x), device_of(y + BY, x)) for y in range(NY) for x in range(NX)]
    return lax.ppermute(value, "xy", moves)


def split3(value):
    high = value.astype(jnp.bfloat16)
    rest = value - high.astype(jnp.float32)
    mid = rest.astype(jnp.bfloat16)
    low = (rest - mid.astype(jnp.float32)).astype(jnp.bfloat16)
    return [high, mid, low]


def with_ones(value):
    ones = jnp.ones((16, value.shape[1]), jnp.bfloat16)
    return jnp.concatenate(split3(value) + [ones], axis=0)


def shifted(device, core):
    return ((device >> 2) + NY - core) & (NY - 1), ((device & (NX - 1)) + NX - core) & (NX - 1)


def near_far(owner, me, core):
    (y, x), (my_y, my_x) = shifted(owner, core), shifted(me, core)
    near_y = (((y + 1) >> 1) + (my_y >> 1)) & 1
    near_x = (((x + 1) >> 1) + (my_x >> 1)) & 1
    place = ((y + 1) & 1) * 2 + ((x + 1) & 1)
    return near_y * 2 + near_x, place * FAR + (y >> 2)


def join3(product, rows):
    return product[2 * rows : 3 * rows] + product[rows : 2 * rows] + product[:rows]


def fetch_all(pairs, sems):
    copies = [pltpu.make_async_copy(src, dst, sems.at[i]) for i, (src, dst) in enumerate(pairs)]
    for copy in copies:
        copy.start()
    return copies


def pinned(value, space):
    return pltpu.with_memory_space_constraint(value, space)


ANY = pl.BlockSpec(memory_space=pl.ANY)
SMEM = pl.BlockSpec(memory_space=pltpu.SMEM)
VMEM = pl.BlockSpec(memory_space=pltpu.VMEM)
PARAMS = pltpu.CompilerParams(vmem_limit_bytes=VMEM_LIMIT)


def small_scratch(lists, owners, starts):
    return [pltpu.SMEM(a.shape, jnp.int32) for a in (lists, owners, starts)]


def fetch_mats(mats_hbm, mats, sems):
    return fetch_all(
        [
            (mats_hbm.at[0, pl.ds(k, MATS_AT_ONCE)], mats.at[pl.ds(k, MATS_AT_ONCE)])
            for k in range(0, mats.shape[0], MATS_AT_ONCE)
        ],
        sems,
    )


def wait_mats(copies, k):
    if k % MATS_AT_ONCE == 0:
        copies[k // MATS_AT_ONCE].wait()


def mats_scratch(mats, others):
    return [
        pltpu.VMEM(mats.shape[1:], jnp.bfloat16),
        pltpu.SemaphoreType.DMA((others,)),
        pltpu.SemaphoreType.DMA((mats.shape[1] // MATS_AT_ONCE,)),
    ]


def project_kernel(
    me_ref, lists_hbm, owners_hbm, starts_hbm, vol_hbm, mats_hbm,
    out_ref, first_ref, last_ref, lists, owners, starts, wide, mats, sems, mat_sems,
):
    rows, cols = vol_hbm.shape
    count = mats.shape[0]
    copies = fetch_all(
        [
            (lists_hbm, lists),
            (owners_hbm, owners),
            (starts_hbm, starts),
            (vol_hbm, wide.at[:, pl.ds(0, cols)]),
        ],
        sems,
    )
    mat_copies = fetch_mats(mats_hbm, mats, mat_sems)
    wide[:, cols:] = jnp.zeros((rows, LANES), jnp.float32)
    out_ref[...] = jnp.zeros(out_ref.shape, jnp.float32)
    for copy in copies:
        copy.wait()
    first_ref[...] = wide[:1, :cols]
    last_ref[...] = wide[rows - 1 :, :cols]
    me, core = me_ref[0], me_ref[1]
    for k in range(count):
        start = starts[0, k]
        near, far = near_far(owners[0, lists[k, me]], me, core)
        base = pl.multiple_of(start & -LANES, LANES)
        window = wide[:, pl.ds(base, W + LANES)]
        window = pltpu.roll(window, (W + LANES) - (start & (LANES - 1)), 1)[:, :W]
        wait_mats(mat_copies, k)
        product = jnp.dot(with_ones(window), mats[k], preferred_element_type=jnp.float32)
        out_ref[near, pl.ds(pl.multiple_of(far * rows, 8), rows), :] = join3(product, rows)
        out_ref[near, pl.ds(SLOTS * rows + far, 1), :] = product[3 * rows : 3 * rows + 1]


def project(me, lists, owners, starts, volume, mats):
    rows, cols = volume.shape
    operands = [pinned(a, pltpu.HBM) for a in (lists, owners, starts, volume, mats)]
    return pl.pallas_call(
        project_kernel,
        out_shape=[
            pltpu.VMEM((QUAD, SLOTS * rows + 8, W), jnp.float32),
            pltpu.VMEM((1, cols), jnp.float32),
            pltpu.VMEM((1, cols), jnp.float32),
        ],
        in_specs=[SMEM] + [ANY] * 5,
        out_specs=[VMEM] * 3,
        scratch_shapes=small_scratch(lists, owners, starts)
        + [pltpu.VMEM((rows, cols + LANES), jnp.float32)]
        + mats_scratch(mats, 4),
        compiler_params=PARAMS,
    )(me, *operands)


def sum_quad(ref):
    return ref[0] + ref[1] + ref[2] + ref[3]


def gather_near_kernel(rows, in_ref, out_ref):
    total = sum_quad(in_ref)
    for place in range(QUAD):
        at = place * FAR
        out_ref[place, : FAR * rows] = total[at * rows : (at + FAR) * rows]
        sums = total[SLOTS * rows + at : SLOTS * rows + at + FAR]
        out_ref[place, FAR * rows : FAR * rows + FAR] = sums
        out_ref[place, FAR * rows + FAR :] = jnp.zeros((8 - FAR, W), jnp.float32)


def gather_near(arrived):
    rows = (arrived.shape[1] - 8) // SLOTS
    return pl.pallas_call(
        functools.partial(gather_near_kernel, rows),
        out_shape=pltpu.VMEM((QUAD, FAR * rows + 8, W), jnp.float32),
        in_specs=[VMEM],
        out_specs=VMEM,
        compiler_params=PARAMS,
    )(pinned(arrived, pltpu.VMEM))


def my_half(me_ref, rows):
    return pl.ds(pl.multiple_of((shifted(me_ref[0], me_ref[1])[0] >> 2) * rows, 8), rows)


def gather_far_kernel(me_ref, in_ref, measured_ref, out_ref):
    rows = measured_ref.shape[0]
    total = sum_quad(in_ref)
    out_ref[: FAR * rows] = -total[: FAR * rows]
    out_ref[FAR * rows :] = total[FAR * rows :]
    mine = my_half(me_ref, rows)
    out_ref[mine, :] = out_ref[mine, :] + measured_ref[...]


def gather_far(me, arrived, measured):
    return pl.pallas_call(
        gather_far_kernel,
        out_shape=pltpu.VMEM(arrived.shape[1:], jnp.float32),
        in_specs=[SMEM, VMEM, VMEM],
        out_specs=VMEM,
        compiler_params=PARAMS,
    )(me, pinned(arrived, pltpu.VMEM), pinned(measured, pltpu.VMEM))


def spread_far_kernel(me_ref, own_ref, came_ref, out_ref, mine_ref):
    rows = mine_ref.shape[0]
    both = own_ref[...] + came_ref[...]
    for half in range(FAR):
        at = FAR * rows + half
        value = both[half * rows : (half + 1) * rows] / both[at : at + 1]
        for place in range(QUAD):
            out_ref[place, half * rows : (half + 1) * rows] = value
    mine_ref[...] = out_ref[0, my_half(me_ref, rows), :]


def spread_far(me, own, came):
    rows = (own.shape[0] - 8) // FAR
    return pl.pallas_call(
        spread_far_kernel,
        out_shape=[
            pltpu.VMEM((QUAD, FAR * rows, W), jnp.float32),
            jax.ShapeDtypeStruct((rows, W), jnp.float32),
        ],
        in_specs=[SMEM, VMEM, VMEM],
        out_specs=[VMEM, VMEM],
        compiler_params=PARAMS,
    )(me, pinned(own, pltpu.VMEM), pinned(came, pltpu.VMEM))


def spread_near_kernel(column_ref, first_in, last_in, out_hbm, first_ref, last_ref, sems):
    copies = fetch_all([(column_ref, out_hbm.at[place]) for place in range(QUAD)], sems)
    first_ref[...] = first_in[...]
    last_ref[...] = last_in[...]
    for copy in copies:
        copy.wait()


def spread_near(column, first, last):
    face = jax.ShapeDtypeStruct(first.shape, jnp.float32)
    return pl.pallas_call(
        spread_near_kernel,
        out_shape=[pltpu.HBM((QUAD,) + column.shape, jnp.float32), face, face],
        in_specs=[VMEM] * 3,
        out_specs=[ANY, VMEM, VMEM],
        scratch_shapes=[pltpu.SemaphoreType.DMA((QUAD,))],
        compiler_params=PARAMS,
    )(*(pinned(a, pltpu.VMEM) for a in (column, first, last)))


def back_kernel(
    me_ref, lists_hbm, owners_hbm, starts_hbm, mats_hbm, base_ref, got_ref, out_ref,
    lists, owners, starts, total, mats, sems, mat_sems,
):
    rows, cols = base_ref.shape
    count = mats.shape[0]
    copies = fetch_all([(lists_hbm, lists), (owners_hbm, owners), (starts_hbm, starts)], sems)
    mat_copies = fetch_mats(mats_hbm, mats, mat_sems)
    total[...] = jnp.zeros(total.shape, jnp.float32)
    for copy in copies:
        copy.wait()
    me, core = me_ref[0], me_ref[1]
    for k in range(count):
        start = starts[0, k]
        near, far = near_far(owners[0, lists[k, me]], me, core)
        base = pl.multiple_of(start & -LANES, LANES)
        wait_mats(mat_copies, k)
        product = lax.dot_general(
            with_ones(got_ref[near, far]),
            mats[k],
            (((1,), (1,)), ((), ())),
            preferred_element_type=jnp.float32,
        )
        value = jnp.concatenate([join3(product, rows), product[3 * rows : 3 * rows + 8]], axis=0)
        value = jnp.concatenate([value, jnp.zeros((rows + 8, LANES), jnp.float32)], axis=1)
        total[:, pl.ds(base, W + LANES)] += pltpu.roll(value, start & (LANES - 1), 1)
    column = jnp.maximum(total[rows : rows + 1, :cols], 1.0)
    out_ref[...] = base_ref[...] + relax * (total[:rows, :cols] / column)


def back_project(me, lists, owners, starts, base, mats, got):
    rows, cols = base.shape
    operands = [pinned(a, pltpu.HBM) for a in (lists, owners, starts, mats)]
    operands += [pinned(a, pltpu.VMEM) for a in (base, got)]
    return pl.pallas_call(
        back_kernel,
        out_shape=jax.ShapeDtypeStruct((rows, cols), jnp.float32),
        in_specs=[SMEM] + [ANY] * 4 + [VMEM] * 2,
        out_specs=VMEM,
        scratch_shapes=small_scratch(lists, owners, starts)
        + [pltpu.VMEM((rows + 8, cols + LANES), jnp.float32)]
        + mats_scratch(mats, 3),
        compiler_params=PARAMS,
    )(me, *operands)


def with_faces(volume, first, last):
    count = lax.axis_size("gz")
    up = [(i, i + 1) for i in range(count - 1)]
    down = [(i + 1, i) for i in range(count - 1)]
    return jnp.concatenate(
        [lax.ppermute(last, "gz", up), volume, lax.ppermute(first, "gz", down)], axis=0
    )


def total_variation(padded):
    diffs = padded[1:] - padded[:-1]
    slopes = diffs / jnp.sqrt(diffs * diffs + smooth_sq)
    return slopes[:-1] - slopes[1:]


def per_device(volume, sinogram, ray_mats, offsets, ray_lists, owner_map):
    rows = volume.shape[0]
    core = lax.axis_index("gz") % 2
    device = lax.axis_index("xy")
    me = jnp.stack([device, core]).astype(jnp.int32)
    plan = (me, ray_lists.T, owner_map.reshape(1, -1), offsets)
    outgoing, first, last = project(*plan, volume, ray_mats)
    part = gather_far(me, exchange(gather_near(exchange(outgoing, 1)), 2), sinogram)
    spread, weighted = spread_far(me, part, swap_far(part))
    column = exchange(spread, 2).reshape(SLOTS, rows, W)
    spread, first, last = spread_near(column, first, last)
    base = volume - tv_weight * total_variation(with_faces(volume, first, last))
    got = exchange(spread, 1)
    new_volume = back_project(*plan, base, ray_mats, got)
    return (new_volume, weighted)


def solution(mesh):
    in_specs = (P("gz", "xy"), P("gz", "xy"), P("xy", None, None, None), P("xy", None), P(), P())
    out_specs = (P("gz", "xy"), P("gz", "xy"))
    return jax.shard_map(
        per_device, mesh=mesh, in_specs=in_specs, out_specs=out_specs, check_vma=False
    )
```

```python
import functools

import jax
import jax.numpy as jnp
from jax import lax
from jax.experimental import pallas as pl
from jax.experimental.pallas import tpu as pltpu
from jax.sharding import PartitionSpec as P

relax = 1.0
tv_weight = 0.2
smooth_sq = 0.01

NX, NY = 4, 8
BX, BY = NX // 2, NY // 2
QUAD, SLOTS, FAR = 4, 8, 2
W = 256
LANES = 128
VMEM_LIMIT = 32 * 1024 * 1024


def device_of(y, x):
    return (y % NY) * NX + x % NX


PLACES = [(qy, qx) for qy in range(2) for qx in range(2)]
BLOCKS = [(by, bx) for by in range(BY) for bx in range(BX)]


def exchange(value, level):
    slabs = lax.axis_size("gz")

    def member(slab, block, place):
        shift = slab % 2 + level - 1
        y, x = 2 * block[0] + place[0] + shift, 2 * block[1] + place[1] + shift
        return device_of(y, x) * slabs + slab

    groups = [
        [member(slab, block, place) for place in PLACES] for slab in range(slabs) for block in BLOCKS
    ]
    return lax.all_to_all(
        value, ("xy", "gz"), split_axis=0, concat_axis=0, axis_index_groups=groups, tiled=True
    )


def swap_far(value):
    moves = [(device_of(y, x), device_of(y + BY, x)) for y in range(NY) for x in range(NX)]
    return lax.ppermute(value, "xy", moves)


def split3(value):
    high = value.astype(jnp.bfloat16)
    rest = value - high.astype(jnp.float32)
    mid = rest.astype(jnp.bfloat16)
    low = (rest - mid.astype(jnp.float32)).astype(jnp.bfloat16)
    return [high, mid, low]


def with_ones(value):
    ones = jnp.ones((16, value.shape[1]), jnp.bfloat16)
    return jnp.concatenate(split3(value) + [ones], axis=0)


def shifted(device, core):
    return ((device >> 2) + NY - core) & (NY - 1), ((device & (NX - 1)) + NX - core) & (NX - 1)


def near_far(owner, me, core):
    (y, x), (my_y, my_x) = shifted(owner, core), shifted(me, core)
    near_y = (((y + 1) >> 1) + (my_y >> 1)) & 1
    near_x = (((x + 1) >> 1) + (my_x >> 1)) & 1
    place = ((y + 1) & 1) * 2 + ((x + 1) & 1)
    return near_y * 2 + near_x, place * FAR + (y >> 2)


def join3(product, rows):
    return product[2 * rows : 3 * rows] + product[rows : 2 * rows] + product[:rows]


def fetch_all(pairs, sems):
    copies = [pltpu.make_async_copy(src, dst, sems.at[i]) for i, (src, dst) in enumerate(pairs)]
    for copy in copies:
        copy.start()
    return copies


def pinned(value, space):
    return pltpu.with_memory_space_constraint(value, space)


ANY = pl.BlockSpec(memory_space=pl.ANY)
SMEM = pl.BlockSpec(memory_space=pltpu.SMEM)
VMEM = pl.BlockSpec(memory_space=pltpu.VMEM)
PARAMS = pltpu.CompilerParams(vmem_limit_bytes=VMEM_LIMIT)


def small_scratch(lists, owners, starts):
    return [pltpu.SMEM(a.shape, jnp.int32) for a in (lists, owners, starts)]


def fetch_mats(mats_hbm, mats, sems):
    size = mats.shape[0] // sems.shape[0]
    return fetch_all(
        [
            (mats_hbm.at[0, pl.ds(k, size)], mats.at[pl.ds(k, size)])
            for k in range(0, mats.shape[0], size)
        ],
        sems,
    )


def wait_mats(copies, k, count):
    size = count // len(copies)
    if k % size == 0:
        copies[k // size].wait()


def mats_scratch(mats, others, pieces):
    return [
        pltpu.VMEM(mats.shape[1:], jnp.bfloat16),
        pltpu.SemaphoreType.DMA((others,)),
        pltpu.SemaphoreType.DMA((pieces,)),
    ]


def project_kernel(
    me_ref, lists_hbm, owners_hbm, starts_hbm, vol_hbm, mats_hbm,
    out_ref, first_ref, last_ref, lists, owners, starts, wide, mats, sems, mat_sems,
):
    rows, cols = vol_hbm.shape
    count = mats.shape[0]
    copies = fetch_all(
        [
            (lists_hbm, lists),
            (owners_hbm, owners),
            (starts_hbm, starts),
            (vol_hbm, wide.at[:, pl.ds(0, cols)]),
        ],
        sems,
    )
    mat_copies = fetch_mats(mats_hbm, mats, mat_sems)
    wide[:, cols:] = jnp.zeros((rows, LANES), jnp.float32)
    out_ref[...] = jnp.zeros(out_ref.shape, jnp.float32)
    for copy in copies:
        copy.wait()
    first_ref[...] = wide[:1, :cols]
    last_ref[...] = wide[rows - 1 :, :cols]
    me, core = me_ref[0], me_ref[1]
    for k in range(count):
        start = starts[0, k]
        near, far = near_far(owners[0, lists[k, me]], me, core)
        base = pl.multiple_of(start & -LANES, LANES)
        window = wide[:, pl.ds(base, W + LANES)]
        window = pltpu.roll(window, (W + LANES) - (start & (LANES - 1)), 1)[:, :W]
        wait_mats(mat_copies, k, count)
        product = jnp.dot(with_ones(window), mats[k], preferred_element_type=jnp.float32)
        out_ref[near, pl.ds(pl.multiple_of(far * rows, 8), rows), :] = join3(product, rows)
        out_ref[near, pl.ds(SLOTS * rows + far, 1), :] = product[3 * rows : 3 * rows + 1]


def project(me, lists, owners, starts, volume, mats):
    rows, cols = volume.shape
    operands = [pinned(a, pltpu.HBM) for a in (lists, owners, starts, volume, mats)]
    return pl.pallas_call(
        project_kernel,
        out_shape=[
            pltpu.VMEM((QUAD, SLOTS * rows + 8, W), jnp.float32),
            pltpu.VMEM((1, cols), jnp.float32),
            pltpu.VMEM((1, cols), jnp.float32),
        ],
        in_specs=[SMEM] + [ANY] * 5,
        out_specs=[VMEM] * 3,
        scratch_shapes=small_scratch(lists, owners, starts)
        + [pltpu.VMEM((rows, cols + LANES), jnp.float32)]
        + mats_scratch(mats, 4, 1),
        compiler_params=PARAMS,
    )(me, *operands)


def sum_quad(ref):
    return ref[0] + ref[1] + ref[2] + ref[3]


def gather_near_kernel(rows, in_ref, out_ref):
    total = sum_quad(in_ref)
    for place in range(QUAD):
        at = place * FAR
        out_ref[place, : FAR * rows] = total[at * rows : (at + FAR) * rows]
        sums = total[SLOTS * rows + at : SLOTS * rows + at + FAR]
        out_ref[place, FAR * rows : FAR * rows + FAR] = sums
        out_ref[place, FAR * rows + FAR :] = jnp.zeros((8 - FAR, W), jnp.float32)


def gather_near(arrived):
    rows = (arrived.shape[1] - 8) // SLOTS
    return pl.pallas_call(
        functools.partial(gather_near_kernel, rows),
        out_shape=pltpu.VMEM((QUAD, FAR * rows + 8, W), jnp.float32),
        in_specs=[VMEM],
        out_specs=VMEM,
        compiler_params=PARAMS,
    )(pinned(arrived, pltpu.VMEM))


def my_half(me_ref, rows):
    return pl.ds(pl.multiple_of((shifted(me_ref[0], me_ref[1])[0] >> 2) * rows, 8), rows)


def gather_far_kernel(me_ref, in_ref, measured_ref, out_ref):
    rows = measured_ref.shape[0]
    total = sum_quad(in_ref)
    out_ref[: FAR * rows] = -total[: FAR * rows]
    out_ref[FAR * rows :] = total[FAR * rows :]
    mine = my_half(me_ref, rows)
    out_ref[mine, :] = out_ref[mine, :] + measured_ref[...]


def gather_far(me, arrived, measured):
    return pl.pallas_call(
        gather_far_kernel,
        out_shape=pltpu.VMEM(arrived.shape[1:], jnp.float32),
        in_specs=[SMEM, VMEM, VMEM],
        out_specs=VMEM,
        compiler_params=PARAMS,
    )(me, pinned(arrived, pltpu.VMEM), pinned(measured, pltpu.VMEM))


def spread_far_kernel(me_ref, own_ref, came_ref, out_ref, mine_ref):
    rows = mine_ref.shape[0]
    both = own_ref[...] + came_ref[...]
    for half in range(FAR):
        at = FAR * rows + half
        value = both[half * rows : (half + 1) * rows] / both[at : at + 1]
        for place in range(QUAD):
            out_ref[place, half * rows : (half + 1) * rows] = value
    mine_ref[...] = out_ref[0, my_half(me_ref, rows), :]


def spread_far(me, own, came):
    rows = (own.shape[0] - 8) // FAR
    return pl.pallas_call(
        spread_far_kernel,
        out_shape=[
            pltpu.VMEM((QUAD, FAR * rows, W), jnp.float32),
            jax.ShapeDtypeStruct((rows, W), jnp.float32),
        ],
        in_specs=[SMEM, VMEM, VMEM],
        out_specs=[VMEM, VMEM],
        compiler_params=PARAMS,
    )(me, pinned(own, pltpu.VMEM), pinned(came, pltpu.VMEM))


def spread_near_kernel(column_ref, first_in, last_in, out_hbm, first_ref, last_ref, sems):
    copies = fetch_all([(column_ref, out_hbm.at[place]) for place in range(QUAD)], sems)
    first_ref[...] = first_in[...]
    last_ref[...] = last_in[...]
    for copy in copies:
        copy.wait()


def spread_near(column, first, last):
    face = jax.ShapeDtypeStruct(first.shape, jnp.float32)
    return pl.pallas_call(
        spread_near_kernel,
        out_shape=[pltpu.HBM((QUAD,) + column.shape, jnp.float32), face, face],
        in_specs=[VMEM] * 3,
        out_specs=[ANY, VMEM, VMEM],
        scratch_shapes=[pltpu.SemaphoreType.DMA((QUAD,))],
        compiler_params=PARAMS,
    )(*(pinned(a, pltpu.VMEM) for a in (column, first, last)))


def back_kernel(
    me_ref, lists_hbm, owners_hbm, starts_hbm, mats_hbm, base_ref, got_ref, out_ref,
    lists, owners, starts, total, mats, sems, mat_sems,
):
    rows, cols = base_ref.shape
    count = mats.shape[0]
    copies = fetch_all([(lists_hbm, lists), (owners_hbm, owners), (starts_hbm, starts)], sems)
    mat_copies = fetch_mats(mats_hbm, mats, mat_sems)
    total[...] = jnp.zeros(total.shape, jnp.float32)
    for copy in copies:
        copy.wait()
    me, core = me_ref[0], me_ref[1]
    for k in range(count):
        start = starts[0, k]
        near, far = near_far(owners[0, lists[k, me]], me, core)
        base = pl.multiple_of(start & -LANES, LANES)
        wait_mats(mat_copies, k, count)
        product = lax.dot_general(
            with_ones(got_ref[near, far]),
            mats[k],
            (((1,), (1,)), ((), ())),
            preferred_element_type=jnp.float32,
        )
        value = jnp.concatenate([join3(product, rows), product[3 * rows : 3 * rows + 8]], axis=0)
        value = jnp.concatenate([value, jnp.zeros((rows + 8, LANES), jnp.float32)], axis=1)
        total[:, pl.ds(base, W + LANES)] += pltpu.roll(value, start & (LANES - 1), 1)
    column = jnp.maximum(total[rows : rows + 1, :cols], 1.0)
    out_ref[...] = base_ref[...] + relax * (total[:rows, :cols] / column)


def back_project(me, lists, owners, starts, base, mats, got):
    rows, cols = base.shape
    operands = [pinned(a, pltpu.HBM) for a in (lists, owners, starts, mats)]
    operands += [pinned(a, pltpu.VMEM) for a in (base, got)]
    return pl.pallas_call(
        back_kernel,
        out_shape=jax.ShapeDtypeStruct((rows, cols), jnp.float32),
        in_specs=[SMEM] + [ANY] * 4 + [VMEM] * 2,
        out_specs=VMEM,
        scratch_shapes=small_scratch(lists, owners, starts)
        + [pltpu.VMEM((rows + 8, cols + LANES), jnp.float32)]
        + mats_scratch(mats, 3, 2),
        compiler_params=PARAMS,
    )(me, *operands)


def with_faces(volume, first, last):
    count = lax.axis_size("gz")
    up = [(i, i + 1) for i in range(count - 1)]
    down = [(i + 1, i) for i in range(count - 1)]
    return jnp.concatenate(
        [lax.ppermute(last, "gz", up), volume, lax.ppermute(first, "gz", down)], axis=0
    )


def total_variation(padded):
    diffs = padded[1:] - padded[:-1]
    slopes = diffs / jnp.sqrt(diffs * diffs + smooth_sq)
    return slopes[:-1] - slopes[1:]


def per_device(volume, sinogram, ray_mats, offsets, ray_lists, owner_map):
    rows = volume.shape[0]
    core = lax.axis_index("gz") % 2
    device = lax.axis_index("xy")
    me = jnp.stack([device, core]).astype(jnp.int32)
    plan = (me, ray_lists.T, owner_map.reshape(1, -1), offsets)
    outgoing, first, last = project(*plan, volume, ray_mats)
    part = gather_far(me, exchange(gather_near(exchange(outgoing, 1)), 2), sinogram)
    spread, weighted = spread_far(me, part, swap_far(part))
    column = exchange(spread, 2).reshape(SLOTS, rows, W)
    spread, first, last = spread_near(column, first, last)
    base = volume - tv_weight * total_variation(with_faces(volume, first, last))
    got = exchange(spread, 1)
    new_volume = back_project(*plan, base, ray_mats, got)
    return (new_volume, weighted)


def solution(mesh):
    in_specs = (P("gz", "xy"), P("gz", "xy"), P("xy", None, None, None), P("xy", None), P(), P())
    out_specs = (P("gz", "xy"), P("gz", "xy"))
    return jax.shard_map(
        per_device, mesh=mesh, in_specs=in_specs, out_specs=out_specs, check_vma=False
    )
```

```python
import functools

import jax
import jax.numpy as jnp
from jax import lax
from jax.experimental import pallas as pl
from jax.experimental.pallas import tpu as pltpu
from jax.sharding import PartitionSpec as P

relax = 1.0
tv_weight = 0.2
smooth_sq = 0.01

NX, NY = 4, 8
BX, BY = NX // 2, NY // 2
QUAD, SLOTS, FAR = 4, 8, 2
W = 256
LANES = 128
VMEM_LIMIT = 32 * 1024 * 1024


def device_of(y, x):
    return (y % NY) * NX + x % NX


PLACES = [(qy, qx) for qy in range(2) for qx in range(2)]
BLOCKS = [(by, bx) for by in range(BY) for bx in range(BX)]


def exchange(value, level):
    slabs = lax.axis_size("gz")

    def member(slab, block, place):
        shift = slab % 2 + level - 1
        y, x = 2 * block[0] + place[0] + shift, 2 * block[1] + place[1] + shift
        return device_of(y, x) * slabs + slab

    groups = [
        [member(slab, block, place) for place in PLACES] for slab in range(slabs) for block in BLOCKS
    ]
    return lax.all_to_all(
        value, ("xy", "gz"), split_axis=0, concat_axis=0, axis_index_groups=groups, tiled=True
    )


def far_partner(y):
    return ((3 if y % 4 in (0, 3) else 7) - y) % NY


def swap_far(value):
    slabs = lax.axis_size("gz")
    moves = [
        (device_of(y + z % 2, x) * slabs + z, device_of(far_partner(y) + z % 2, x) * slabs + z)
        for y in range(NY)
        for x in range(NX)
        for z in range(slabs)
    ]
    return lax.ppermute(value, ("xy", "gz"), moves)


def split3(value):
    high = value.astype(jnp.bfloat16)
    rest = value - high.astype(jnp.float32)
    mid = rest.astype(jnp.bfloat16)
    low = (rest - mid.astype(jnp.float32)).astype(jnp.bfloat16)
    return [high, mid, low]


def with_ones(value):
    ones = jnp.ones((16, value.shape[1]), jnp.bfloat16)
    return jnp.concatenate(split3(value) + [ones], axis=0)


def shifted(device, core):
    return ((device >> 2) + NY - core) & (NY - 1), ((device & (NX - 1)) + NX - core) & (NX - 1)


def near_far(owner, me, core):
    (y, x), (my_y, my_x) = shifted(owner, core), shifted(me, core)
    inner = ((y + 1) >> 1) & 1
    near_y = inner ^ ((my_y >> 1) & 1)
    upper = (y >> 2) ^ (inner & (y >> 1) & 1)
    far_side = (((my_y & 6) + near_y + NY - 1) & (NY - 1)) >> 2
    near_x = (((x + 1) >> 1) + (my_x >> 1)) & 1
    place = (upper ^ far_side) * 2 + ((x + 1) & 1)
    return near_y * 2 + near_x, place * FAR + (y & 1)


def join3(product, rows):
    return product[2 * rows : 3 * rows] + product[rows : 2 * rows] + product[:rows]


def fetch_all(pairs, sems):
    copies = [pltpu.make_async_copy(src, dst, sems.at[i]) for i, (src, dst) in enumerate(pairs)]
    for copy in copies:
        copy.start()
    return copies


def pinned(value, space):
    return pltpu.with_memory_space_constraint(value, space)


ANY = pl.BlockSpec(memory_space=pl.ANY)
SMEM = pl.BlockSpec(memory_space=pltpu.SMEM)
VMEM = pl.BlockSpec(memory_space=pltpu.VMEM)
PARAMS = pltpu.CompilerParams(vmem_limit_bytes=VMEM_LIMIT)


def small_scratch(lists, owners, starts):
    return [pltpu.SMEM(a.shape, jnp.int32) for a in (lists, owners, starts)]


def fetch_mats(mats_hbm, mats, sems):
    size = mats.shape[0] // sems.shape[0]
    return fetch_all(
        [
            (mats_hbm.at[0, pl.ds(k, size)], mats.at[pl.ds(k, size)])
            for k in range(0, mats.shape[0], size)
        ],
        sems,
    )


def wait_mats(copies, k, count):
    size = count // len(copies)
    if k % size == 0:
        copies[k // size].wait()


def mats_scratch(mats, others, pieces):
    return [
        pltpu.VMEM(mats.shape[1:], jnp.bfloat16),
        pltpu.SemaphoreType.DMA((others,)),
        pltpu.SemaphoreType.DMA((pieces,)),
    ]


def project_kernel(
    me_ref, lists_hbm, owners_hbm, starts_hbm, vol_hbm, mats_hbm,
    out_ref, first_ref, last_ref, lists, owners, starts, wide, mats, sems, mat_sems,
):
    rows, cols = vol_hbm.shape
    count = mats.shape[0]
    copies = fetch_all(
        [
            (lists_hbm, lists),
            (owners_hbm, owners),
            (starts_hbm, starts),
            (vol_hbm, wide.at[:, pl.ds(0, cols)]),
        ],
        sems,
    )
    mat_copies = fetch_mats(mats_hbm, mats, mat_sems)
    wide[:, cols:] = jnp.zeros((rows, LANES), jnp.float32)
    out_ref[...] = jnp.zeros(out_ref.shape, jnp.float32)
    for copy in copies:
        copy.wait()
    first_ref[...] = wide[:1, :cols]
    last_ref[...] = wide[rows - 1 :, :cols]
    me, core = me_ref[0], me_ref[1]
    for k in range(count):
        start = starts[0, k]
        near, far = near_far(owners[0, lists[k, me]], me, core)
        base = pl.multiple_of(start & -LANES, LANES)
        window = wide[:, pl.ds(base, W + LANES)]
        window = pltpu.roll(window, (W + LANES) - (start & (LANES - 1)), 1)[:, :W]
        wait_mats(mat_copies, k, count)
        product = jnp.dot(with_ones(window), mats[k], preferred_element_type=jnp.float32)
        out_ref[near, pl.ds(pl.multiple_of(far * rows, 8), rows), :] = join3(product, rows)
        out_ref[near, pl.ds(SLOTS * rows + far, 1), :] = product[3 * rows : 3 * rows + 1]


def project(me, lists, owners, starts, volume, mats):
    rows, cols = volume.shape
    operands = [pinned(a, pltpu.HBM) for a in (lists, owners, starts, volume, mats)]
    return pl.pallas_call(
        project_kernel,
        out_shape=[
            pltpu.VMEM((QUAD, SLOTS * rows + 8, W), jnp.float32),
            pltpu.VMEM((1, cols), jnp.float32),
            pltpu.VMEM((1, cols), jnp.float32),
        ],
        in_specs=[SMEM] + [ANY] * 5,
        out_specs=[VMEM] * 3,
        scratch_shapes=small_scratch(lists, owners, starts)
        + [pltpu.VMEM((rows, cols + LANES), jnp.float32)]
        + mats_scratch(mats, 4, 1),
        compiler_params=PARAMS,
    )(me, *operands)


def sum_quad(ref):
    return ref[0] + ref[1] + ref[2] + ref[3]


def gather_near_kernel(rows, in_ref, out_ref):
    total = sum_quad(in_ref)
    for place in range(QUAD):
        at = place * FAR
        out_ref[place, : FAR * rows] = total[at * rows : (at + FAR) * rows]
        sums = total[SLOTS * rows + at : SLOTS * rows + at + FAR]
        out_ref[place, FAR * rows : FAR * rows + FAR] = sums
        out_ref[place, FAR * rows + FAR :] = jnp.zeros((8 - FAR, W), jnp.float32)


def gather_near(arrived):
    rows = (arrived.shape[1] - 8) // SLOTS
    return pl.pallas_call(
        functools.partial(gather_near_kernel, rows),
        out_shape=pltpu.VMEM((QUAD, FAR * rows + 8, W), jnp.float32),
        in_specs=[VMEM],
        out_specs=VMEM,
        compiler_params=PARAMS,
    )(pinned(arrived, pltpu.VMEM))


def my_half(me_ref, rows):
    return pl.ds(pl.multiple_of((shifted(me_ref[0], me_ref[1])[0] & 1) * rows, 8), rows)


def gather_far_kernel(me_ref, in_ref, measured_ref, out_ref):
    rows = measured_ref.shape[0]
    total = sum_quad(in_ref)
    out_ref[: FAR * rows] = -total[: FAR * rows]
    out_ref[FAR * rows :] = total[FAR * rows :]
    mine = my_half(me_ref, rows)
    out_ref[mine, :] = out_ref[mine, :] + measured_ref[...]


def gather_far(me, arrived, measured):
    return pl.pallas_call(
        gather_far_kernel,
        out_shape=pltpu.VMEM(arrived.shape[1:], jnp.float32),
        in_specs=[SMEM, VMEM, VMEM],
        out_specs=VMEM,
        compiler_params=PARAMS,
    )(me, pinned(arrived, pltpu.VMEM), pinned(measured, pltpu.VMEM))


def spread_far_kernel(me_ref, own_ref, came_ref, out_ref, mine_ref):
    rows = mine_ref.shape[0]
    both = own_ref[...] + came_ref[...]
    for half in range(FAR):
        at = FAR * rows + half
        value = both[half * rows : (half + 1) * rows] / both[at : at + 1]
        for place in range(QUAD):
            out_ref[place, half * rows : (half + 1) * rows] = value
    mine_ref[...] = out_ref[0, my_half(me_ref, rows), :]


def spread_far(me, own, came):
    rows = (own.shape[0] - 8) // FAR
    return pl.pallas_call(
        spread_far_kernel,
        out_shape=[
            pltpu.VMEM((QUAD, FAR * rows, W), jnp.float32),
            jax.ShapeDtypeStruct((rows, W), jnp.float32),
        ],
        in_specs=[SMEM, VMEM, VMEM],
        out_specs=[VMEM, VMEM],
        compiler_params=PARAMS,
    )(me, pinned(own, pltpu.VMEM), pinned(came, pltpu.VMEM))


def spread_near_kernel(column_ref, first_in, last_in, out_hbm, first_ref, last_ref, sems):
    copies = fetch_all([(column_ref, out_hbm.at[place]) for place in range(QUAD)], sems)
    first_ref[...] = first_in[...]
    last_ref[...] = last_in[...]
    for copy in copies:
        copy.wait()


def spread_near(column, first, last):
    face = jax.ShapeDtypeStruct(first.shape, jnp.float32)
    return pl.pallas_call(
        spread_near_kernel,
        out_shape=[pltpu.HBM((QUAD,) + column.shape, jnp.float32), face, face],
        in_specs=[VMEM] * 3,
        out_specs=[ANY, VMEM, VMEM],
        scratch_shapes=[pltpu.SemaphoreType.DMA((QUAD,))],
        compiler_params=PARAMS,
    )(*(pinned(a, pltpu.VMEM) for a in (column, first, last)))


def back_kernel(
    me_ref, lists_hbm, owners_hbm, starts_hbm, mats_hbm, base_ref, got_ref, out_ref,
    lists, owners, starts, total, mats, sems, mat_sems,
):
    rows, cols = base_ref.shape
    count = mats.shape[0]
    copies = fetch_all([(lists_hbm, lists), (owners_hbm, owners), (starts_hbm, starts)], sems)
    mat_copies = fetch_mats(mats_hbm, mats, mat_sems)
    total[...] = jnp.zeros(total.shape, jnp.float32)
    for copy in copies:
        copy.wait()
    me, core = me_ref[0], me_ref[1]
    for k in range(count):
        start = starts[0, k]
        near, far = near_far(owners[0, lists[k, me]], me, core)
        base = pl.multiple_of(start & -LANES, LANES)
        wait_mats(mat_copies, k, count)
        product = lax.dot_general(
            with_ones(got_ref[near, far]),
            mats[k],
            (((1,), (1,)), ((), ())),
            preferred_element_type=jnp.float32,
        )
        value = jnp.concatenate([join3(product, rows), product[3 * rows : 3 * rows + 8]], axis=0)
        value = jnp.concatenate([value, jnp.zeros((rows + 8, LANES), jnp.float32)], axis=1)
        total[:, pl.ds(base, W + LANES)] += pltpu.roll(value, start & (LANES - 1), 1)
    column = jnp.maximum(total[rows : rows + 1, :cols], 1.0)
    out_ref[...] = base_ref[...] + relax * (total[:rows, :cols] / column)


def back_project(me, lists, owners, starts, base, mats, got):
    rows, cols = base.shape
    operands = [pinned(a, pltpu.HBM) for a in (lists, owners, starts, mats)]
    operands += [pinned(a, pltpu.VMEM) for a in (base, got)]
    return pl.pallas_call(
        back_kernel,
        out_shape=jax.ShapeDtypeStruct((rows, cols), jnp.float32),
        in_specs=[SMEM] + [ANY] * 4 + [VMEM] * 2,
        out_specs=VMEM,
        scratch_shapes=small_scratch(lists, owners, starts)
        + [pltpu.VMEM((rows + 8, cols + LANES), jnp.float32)]
        + mats_scratch(mats, 3, 2),
        compiler_params=PARAMS,
    )(me, *operands)


def with_faces(volume, first, last):
    count = lax.axis_size("gz")
    up = [(i, i + 1) for i in range(count - 1)]
    down = [(i + 1, i) for i in range(count - 1)]
    return jnp.concatenate(
        [lax.ppermute(last, "gz", up), volume, lax.ppermute(first, "gz", down)], axis=0
    )


def total_variation(padded):
    diffs = padded[1:] - padded[:-1]
    slopes = diffs / jnp.sqrt(diffs * diffs + smooth_sq)
    return slopes[:-1] - slopes[1:]


def per_device(volume, sinogram, ray_mats, offsets, ray_lists, owner_map):
    rows = volume.shape[0]
    core = lax.axis_index("gz") % 2
    device = lax.axis_index("xy")
    me = jnp.stack([device, core]).astype(jnp.int32)
    plan = (me, ray_lists.T, owner_map.reshape(1, -1), offsets)
    outgoing, first, last = project(*plan, volume, ray_mats)
    part = gather_far(me, exchange(gather_near(exchange(outgoing, 1)), 2), sinogram)
    spread, weighted = spread_far(me, part, swap_far(part))
    column = exchange(spread, 2).reshape(SLOTS, rows, W)
    spread, first, last = spread_near(column, first, last)
    base = volume - tv_weight * total_variation(with_faces(volume, first, last))
    got = exchange(spread, 1)
    new_volume = back_project(*plan, base, ray_mats, got)
    return (new_volume, weighted)


def solution(mesh):
    in_specs = (P("gz", "xy"), P("gz", "xy"), P("xy", None, None, None), P("xy", None), P(), P())
    out_specs = (P("gz", "xy"), P("gz", "xy"))
    return jax.shard_map(
        per_device, mesh=mesh, in_specs=in_specs, out_specs=out_specs, check_vma=False
    )
```

```python
import functools

import jax
import jax.numpy as jnp
from jax import lax
from jax.experimental import pallas as pl
from jax.experimental.pallas import tpu as pltpu
from jax.sharding import PartitionSpec as P

relax = 1.0
tv_weight = 0.2
smooth_sq = 0.01

NX, NY = 4, 8
BX, BY = NX // 2, NY // 2
QUAD, SLOTS, FAR = 4, 8, 2
W = 256
LANES = 128
VMEM_LIMIT = 32 * 1024 * 1024


def device_of(y, x):
    return (y % NY) * NX + x % NX


PLACES = [(qy, qx) for qy in range(2) for qx in range(2)]
BLOCKS = [(by, bx) for by in range(BY) for bx in range(BX)]


def exchange(value, level):
    slabs = lax.axis_size("gz")

    def member(slab, block, place):
        shift = slab % 2 + level - 1
        y, x = 2 * block[0] + place[0] + shift, 2 * block[1] + place[1] + shift
        return device_of(y, x) * slabs + slab

    groups = [
        [member(slab, block, place) for place in PLACES] for slab in range(slabs) for block in BLOCKS
    ]
    return lax.all_to_all(
        value, ("xy", "gz"), split_axis=0, concat_axis=0, axis_index_groups=groups, tiled=True
    )


def far_partner(y):
    return ((3 if y % 4 in (0, 3) else 7) - y) % NY


def swap_far(value):
    slabs = lax.axis_size("gz")
    moves = [
        (device_of(y + z % 2, x) * slabs + z, device_of(far_partner(y) + z % 2, x) * slabs + z)
        for y in range(NY)
        for x in range(NX)
        for z in range(slabs)
    ]
    return lax.ppermute(value, ("xy", "gz"), moves)


def split3(value):
    high = value.astype(jnp.bfloat16)
    rest = value - high.astype(jnp.float32)
    mid = rest.astype(jnp.bfloat16)
    low = (rest - mid.astype(jnp.float32)).astype(jnp.bfloat16)
    return [high, mid, low]


def with_ones(value):
    ones = jnp.ones((16, value.shape[1]), jnp.bfloat16)
    return jnp.concatenate(split3(value) + [ones], axis=0)


def shifted(device, core):
    return ((device >> 2) + NY - core) & (NY - 1), ((device & (NX - 1)) + NX - core) & (NX - 1)


def near_far(owner, me, core):
    (y, x), (my_y, my_x) = shifted(owner, core), shifted(me, core)
    inner = ((y + 1) >> 1) & 1
    near_y = inner ^ ((my_y >> 1) & 1)
    upper = (y >> 2) ^ (inner & (y >> 1) & 1)
    far_side = (((my_y & 6) + near_y + NY - 1) & (NY - 1)) >> 2
    near_x = (((x + 1) >> 1) + (my_x >> 1)) & 1
    place = (upper ^ far_side) * 2 + ((x + 1) & 1)
    return near_y * 2 + near_x, place * FAR + (y & 1)


def join3(product, rows):
    return product[2 * rows : 3 * rows] + product[rows : 2 * rows] + product[:rows]


def fetch_all(pairs, sems):
    copies = [pltpu.make_async_copy(src, dst, sems.at[i]) for i, (src, dst) in enumerate(pairs)]
    for copy in copies:
        copy.start()
    return copies


def pinned(value, space):
    return pltpu.with_memory_space_constraint(value, space)


ANY = pl.BlockSpec(memory_space=pl.ANY)
SMEM = pl.BlockSpec(memory_space=pltpu.SMEM)
VMEM = pl.BlockSpec(memory_space=pltpu.VMEM)
PARAMS = pltpu.CompilerParams(vmem_limit_bytes=VMEM_LIMIT)


def small_scratch(lists, owners, starts):
    return [pltpu.SMEM(a.shape, jnp.int32) for a in (lists, owners, starts)]


def fetch_mats(mats_hbm, mats, sems):
    size = mats.shape[0] // sems.shape[0]
    return fetch_all(
        [
            (mats_hbm.at[0, pl.ds(k, size)], mats.at[pl.ds(k, size)])
            for k in range(0, mats.shape[0], size)
        ],
        sems,
    )


def wait_mats(copies, k, count):
    size = count // len(copies)
    if k % size == 0:
        copies[k // size].wait()


def mats_scratch(mats, others, pieces):
    return [
        pltpu.VMEM(mats.shape[1:], jnp.bfloat16),
        pltpu.SemaphoreType.DMA((others,)),
        pltpu.SemaphoreType.DMA((pieces,)),
    ]


def project_kernel(
    me_ref, lists_hbm, owners_hbm, starts_hbm, vol_hbm, mats_hbm,
    out_ref, first_ref, last_ref, lists, owners, starts, wide, mats, sems, mat_sems,
):
    rows, cols = vol_hbm.shape
    count = mats.shape[0]
    copies = fetch_all(
        [
            (lists_hbm, lists),
            (owners_hbm, owners),
            (starts_hbm, starts),
            (vol_hbm, wide.at[:, pl.ds(0, cols)]),
        ],
        sems,
    )
    mat_copies = fetch_mats(mats_hbm, mats, mat_sems)
    wide[:, cols:] = jnp.zeros((rows, LANES), jnp.float32)
    out_ref[...] = jnp.zeros(out_ref.shape, jnp.float32)
    for copy in copies:
        copy.wait()
    first_ref[...] = wide[:1, :cols]
    last_ref[...] = wide[rows - 1 :, :cols]
    me, core = me_ref[0], me_ref[1]
    for k in range(count):
        start = starts[0, k]
        near, far = near_far(owners[0, lists[k, me]], me, core)
        base = pl.multiple_of(start & -LANES, LANES)
        window = wide[:, pl.ds(base, W + LANES)]
        window = pltpu.roll(window, (W + LANES) - (start & (LANES - 1)), 1)[:, :W]
        wait_mats(mat_copies, k, count)
        product = jnp.dot(with_ones(window), mats[k], preferred_element_type=jnp.float32)
        out_ref[near, pl.ds(pl.multiple_of(far * rows, 8), rows), :] = join3(product, rows)
        out_ref[near, pl.ds(SLOTS * rows + far, 1), :] = product[3 * rows : 3 * rows + 1]


def project(me, lists, owners, starts, volume, mats):
    rows, cols = volume.shape
    operands = [pinned(a, pltpu.HBM) for a in (lists, owners, starts, volume, mats)]
    return pl.pallas_call(
        project_kernel,
        out_shape=[
            pltpu.VMEM((QUAD, SLOTS * rows + 8, W), jnp.float32),
            pltpu.VMEM((1, cols), jnp.float32),
            pltpu.VMEM((1, cols), jnp.float32),
        ],
        in_specs=[SMEM] + [ANY] * 5,
        out_specs=[VMEM] * 3,
        scratch_shapes=small_scratch(lists, owners, starts)
        + [pltpu.VMEM((rows, cols + LANES), jnp.float32)]
        + mats_scratch(mats, 4, 1),
        compiler_params=PARAMS,
    )(me, *operands)


def sum_quad(ref):
    return ref[0] + ref[1] + ref[2] + ref[3]


def gather_near_kernel(rows, in_ref, out_ref):
    total = sum_quad(in_ref)
    for place in range(QUAD):
        at = place * FAR
        out_ref[place, : FAR * rows] = total[at * rows : (at + FAR) * rows]
        sums = total[SLOTS * rows + at : SLOTS * rows + at + FAR]
        out_ref[place, FAR * rows : FAR * rows + FAR] = sums
        out_ref[place, FAR * rows + FAR :] = jnp.zeros((8 - FAR, W), jnp.float32)


def gather_near(arrived):
    rows = (arrived.shape[1] - 8) // SLOTS
    return pl.pallas_call(
        functools.partial(gather_near_kernel, rows),
        out_shape=pltpu.VMEM((QUAD, FAR * rows + 8, W), jnp.float32),
        in_specs=[VMEM],
        out_specs=VMEM,
        compiler_params=PARAMS,
    )(pinned(arrived, pltpu.VMEM))


def my_half(me_ref, rows):
    return pl.ds(pl.multiple_of((shifted(me_ref[0], me_ref[1])[0] & 1) * rows, 8), rows)


def gather_far_kernel(me_ref, in_ref, measured_ref, out_ref):
    rows = measured_ref.shape[0]
    total = sum_quad(in_ref)
    out_ref[: FAR * rows] = -total[: FAR * rows]
    out_ref[FAR * rows :] = total[FAR * rows :]
    mine = my_half(me_ref, rows)
    out_ref[mine, :] = out_ref[mine, :] + measured_ref[...]


def gather_far(me, arrived, measured):
    return pl.pallas_call(
        gather_far_kernel,
        out_shape=pltpu.VMEM(arrived.shape[1:], jnp.float32),
        in_specs=[SMEM, VMEM, VMEM],
        out_specs=VMEM,
        compiler_params=PARAMS,
    )(me, pinned(arrived, pltpu.VMEM), pinned(measured, pltpu.VMEM))


def spread_far_kernel(own_ref, came_ref, out_ref):
    rows = out_ref.shape[1] // FAR
    both = own_ref[...] + came_ref[...]
    for half in range(FAR):
        at = FAR * rows + half
        value = both[half * rows : (half + 1) * rows] / both[at : at + 1]
        for place in range(QUAD):
            out_ref[place, half * rows : (half + 1) * rows] = value


def spread_far(own, came):
    rows = (own.shape[0] - 8) // FAR
    return pl.pallas_call(
        spread_far_kernel,
        out_shape=pltpu.VMEM((QUAD, FAR * rows, W), jnp.float32),
        in_specs=[VMEM, VMEM],
        out_specs=VMEM,
        compiler_params=PARAMS,
    )(pinned(own, pltpu.VMEM), pinned(came, pltpu.VMEM))


def spread_near_kernel(
    me_ref, column_ref, far_ref, first_in, last_in, out_hbm, mine_hbm, first_ref, last_ref, sems
):
    mine = far_ref.at[0, my_half(me_ref, mine_hbm.shape[0])]
    copies = fetch_all(
        [(column_ref, out_hbm.at[place]) for place in range(QUAD)] + [(mine, mine_hbm)], sems
    )
    first_ref[...] = first_in[...]
    last_ref[...] = last_in[...]
    for copy in copies:
        copy.wait()


def spread_near(me, column, far, first, last):
    face = jax.ShapeDtypeStruct(first.shape, jnp.float32)
    return pl.pallas_call(
        spread_near_kernel,
        out_shape=[
            pltpu.HBM((QUAD,) + column.shape, jnp.float32),
            pltpu.HBM(column.shape[1:], jnp.float32),
            face,
            face,
        ],
        in_specs=[SMEM] + [VMEM] * 4,
        out_specs=[ANY, ANY, VMEM, VMEM],
        scratch_shapes=[pltpu.SemaphoreType.DMA((QUAD + 1,))],
        compiler_params=PARAMS,
    )(me, *(pinned(a, pltpu.VMEM) for a in (column, far, first, last)))


def back_kernel(
    me_ref, lists_hbm, owners_hbm, starts_hbm, mats_hbm, base_ref, got_ref, out_ref,
    lists, owners, starts, total, mats, sems, mat_sems,
):
    rows, cols = base_ref.shape
    count = mats.shape[0]
    copies = fetch_all([(lists_hbm, lists), (owners_hbm, owners), (starts_hbm, starts)], sems)
    mat_copies = fetch_mats(mats_hbm, mats, mat_sems)
    total[...] = jnp.zeros(total.shape, jnp.float32)
    for copy in copies:
        copy.wait()
    me, core = me_ref[0], me_ref[1]
    for k in range(count):
        start = starts[0, k]
        near, far = near_far(owners[0, lists[k, me]], me, core)
        base = pl.multiple_of(start & -LANES, LANES)
        wait_mats(mat_copies, k, count)
        product = lax.dot_general(
            with_ones(got_ref[near, far]),
            mats[k],
            (((1,), (1,)), ((), ())),
            preferred_element_type=jnp.float32,
        )
        value = jnp.concatenate([join3(product, rows), product[3 * rows : 3 * rows + 8]], axis=0)
        value = jnp.concatenate([value, jnp.zeros((rows + 8, LANES), jnp.float32)], axis=1)
        total[:, pl.ds(base, W + LANES)] += pltpu.roll(value, start & (LANES - 1), 1)
    column = jnp.maximum(total[rows : rows + 1, :cols], 1.0)
    out_ref[...] = base_ref[...] + relax * (total[:rows, :cols] / column)


def back_project(me, lists, owners, starts, base, mats, got):
    rows, cols = base.shape
    operands = [pinned(a, pltpu.HBM) for a in (lists, owners, starts, mats)]
    operands += [pinned(a, pltpu.VMEM) for a in (base, got)]
    return pl.pallas_call(
        back_kernel,
        out_shape=jax.ShapeDtypeStruct((rows, cols), jnp.float32),
        in_specs=[SMEM] + [ANY] * 4 + [VMEM] * 2,
        out_specs=VMEM,
        scratch_shapes=small_scratch(lists, owners, starts)
        + [pltpu.VMEM((rows + 8, cols + LANES), jnp.float32)]
        + mats_scratch(mats, 3, 2),
        compiler_params=PARAMS,
    )(me, *operands)


def with_faces(volume, first, last):
    count = lax.axis_size("gz")
    up = [(i, i + 1) for i in range(count - 1)]
    down = [(i + 1, i) for i in range(count - 1)]
    return jnp.concatenate(
        [lax.ppermute(last, "gz", up), volume, lax.ppermute(first, "gz", down)], axis=0
    )


def total_variation(padded):
    diffs = padded[1:] - padded[:-1]
    slopes = diffs / jnp.sqrt(diffs * diffs + smooth_sq)
    return slopes[:-1] - slopes[1:]


def per_device(volume, sinogram, ray_mats, offsets, ray_lists, owner_map):
    rows = volume.shape[0]
    core = lax.axis_index("gz") % 2
    device = lax.axis_index("xy")
    me = jnp.stack([device, core]).astype(jnp.int32)
    plan = (me, ray_lists.T, owner_map.reshape(1, -1), offsets)
    outgoing, first, last = project(*plan, volume, ray_mats)
    part = gather_far(me, exchange(gather_near(exchange(outgoing, 1)), 2), sinogram)
    far = spread_far(part, swap_far(part))
    column = exchange(far, 2).reshape(SLOTS, rows, W)
    spread, weighted, first, last = spread_near(me, column, far, first, last)
    base = volume - tv_weight * total_variation(with_faces(volume, first, last))
    got = exchange(spread, 1)
    new_volume = back_project(*plan, base, ray_mats, got)
    return (new_volume, weighted)


def solution(mesh):
    in_specs = (P("gz", "xy"), P("gz", "xy"), P("xy", None, None, None), P("xy", None), P(), P())
    out_specs = (P("gz", "xy"), P("gz", "xy"))
    return jax.shard_map(
        per_device, mesh=mesh, in_specs=in_specs, out_specs=out_specs, check_vma=False
    )
```

```python
import functools

import jax
import jax.numpy as jnp
from jax import lax
from jax.experimental import pallas as pl
from jax.experimental.pallas import tpu as pltpu
from jax.sharding import PartitionSpec as P

relax = 1.0
tv_weight = 0.2
smooth_sq = 0.01

NX, NY = 4, 8
BX, BY = NX // 2, NY // 2
QUAD, SLOTS, FAR = 4, 8, 2
W = 256
LANES = 128
VMEM_LIMIT = 32 * 1024 * 1024


def device_of(y, x):
    return (y % NY) * NX + x % NX


PLACES = [(qy, qx) for qy in range(2) for qx in range(2)]
BLOCKS = [(by, bx) for by in range(BY) for bx in range(BX)]


def exchange(value, level):
    slabs = lax.axis_size("gz")

    def member(slab, block, place):
        shift = slab % 2 + level - 1
        y, x = 2 * block[0] + place[0] + shift, 2 * block[1] + place[1] + shift
        return device_of(y, x) * slabs + slab

    groups = [
        [member(slab, block, place) for place in PLACES] for slab in range(slabs) for block in BLOCKS
    ]
    return lax.all_to_all(
        value, ("xy", "gz"), split_axis=0, concat_axis=0, axis_index_groups=groups, tiled=True
    )


def far_partner(y):
    return ((3 if y % 4 in (0, 3) else 7) - y) % NY


def swap_far(value):
    slabs = lax.axis_size("gz")
    moves = [
        (device_of(y + z % 2, x) * slabs + z, device_of(far_partner(y) + z % 2, x) * slabs + z)
        for y in range(NY)
        for x in range(NX)
        for z in range(slabs)
    ]
    return lax.ppermute(value, ("xy", "gz"), moves)


def split3(value):
    high = value.astype(jnp.bfloat16)
    rest = value - high.astype(jnp.float32)
    mid = rest.astype(jnp.bfloat16)
    low = (rest - mid.astype(jnp.float32)).astype(jnp.bfloat16)
    return [high, mid, low]


def with_ones(value):
    ones = jnp.ones((16, value.shape[1]), jnp.bfloat16)
    return jnp.concatenate(split3(value) + [ones], axis=0)


def shifted(device, core):
    return ((device >> 2) + NY - core) & (NY - 1), ((device & (NX - 1)) + NX - core) & (NX - 1)


def near_far(owner, me, core):
    (y, x), (my_y, my_x) = shifted(owner, core), shifted(me, core)
    inner = ((y + 1) >> 1) & 1
    near_y = inner ^ ((my_y >> 1) & 1)
    upper = (y >> 2) ^ (inner & (y >> 1) & 1)
    far_side = (((my_y & 6) + near_y + NY - 1) & (NY - 1)) >> 2
    near_x = (((x + 1) >> 1) + (my_x >> 1)) & 1
    place = (upper ^ far_side) * 2 + ((x + 1) & 1)
    return near_y * 2 + near_x, place * FAR + (y & 1)


def join3(product, rows):
    return product[2 * rows : 3 * rows] + product[rows : 2 * rows] + product[:rows]


def fetch_all(pairs, sems):
    copies = [pltpu.make_async_copy(src, dst, sems.at[i]) for i, (src, dst) in enumerate(pairs)]
    for copy in copies:
        copy.start()
    return copies


def pinned(value, space):
    return pltpu.with_memory_space_constraint(value, space)


ANY = pl.BlockSpec(memory_space=pl.ANY)
SMEM = pl.BlockSpec(memory_space=pltpu.SMEM)
VMEM = pl.BlockSpec(memory_space=pltpu.VMEM)
PARAMS = pltpu.CompilerParams(vmem_limit_bytes=VMEM_LIMIT)


def small_scratch(lists, owners, starts):
    return [pltpu.SMEM(a.shape, jnp.int32) for a in (lists, owners, starts)]


def fetch_mats(mats_hbm, mats, sems):
    size = mats.shape[0] // sems.shape[0]
    return fetch_all(
        [
            (mats_hbm.at[0, pl.ds(k, size)], mats.at[pl.ds(k, size)])
            for k in range(0, mats.shape[0], size)
        ],
        sems,
    )


def wait_mats(copies, k, count):
    size = count // len(copies)
    if k % size == 0:
        copies[k // size].wait()


def mats_scratch(mats, others, pieces):
    return [
        pltpu.VMEM(mats.shape[1:], jnp.bfloat16),
        pltpu.SemaphoreType.DMA((others,)),
        pltpu.SemaphoreType.DMA((pieces,)),
    ]


def project_kernel(
    me_ref, lists_hbm, owners_hbm, starts_hbm, vol_hbm, mats_hbm,
    out_ref, first_ref, last_ref, lists, owners, starts, wide, mats, sems, mat_sems,
):
    rows, cols = vol_hbm.shape
    count = mats.shape[0]
    copies = fetch_all(
        [
            (lists_hbm, lists),
            (owners_hbm, owners),
            (starts_hbm, starts),
            (vol_hbm, wide.at[:, pl.ds(0, cols)]),
        ],
        sems,
    )
    mat_copies = fetch_mats(mats_hbm, mats, mat_sems)
    wide[:, cols:] = jnp.zeros((rows, LANES), jnp.float32)
    out_ref[...] = jnp.zeros(out_ref.shape, jnp.float32)
    for copy in copies:
        copy.wait()
    first_ref[...] = wide[:1, :cols]
    last_ref[...] = wide[rows - 1 :, :cols]
    me, core = me_ref[0], me_ref[1]
    for k in range(count):
        start = starts[0, k]
        near, far = near_far(owners[0, lists[k, me]], me, core)
        base = pl.multiple_of(start & -LANES, LANES)
        window = wide[:, pl.ds(base, W + LANES)]
        window = pltpu.roll(window, (W + LANES) - (start & (LANES - 1)), 1)[:, :W]
        wait_mats(mat_copies, k, count)
        product = jnp.dot(with_ones(window), mats[k], preferred_element_type=jnp.float32)
        out_ref[near, pl.ds(pl.multiple_of(far * rows, 8), rows), :] = join3(product, rows)
        out_ref[near, pl.ds(SLOTS * rows + far, 1), :] = product[3 * rows : 3 * rows + 1]


def project(me, lists, owners, starts, volume, mats):
    rows, cols = volume.shape
    operands = [pinned(a, pltpu.HBM) for a in (lists, owners, starts, volume, mats)]
    return pl.pallas_call(
        project_kernel,
        out_shape=[
            pltpu.VMEM((QUAD, SLOTS * rows + 8, W), jnp.float32),
            pltpu.VMEM((1, cols), jnp.float32),
            pltpu.VMEM((1, cols), jnp.float32),
        ],
        in_specs=[SMEM] + [ANY] * 5,
        out_specs=[VMEM] * 3,
        scratch_shapes=small_scratch(lists, owners, starts)
        + [pltpu.VMEM((rows, cols + LANES), jnp.float32)]
        + mats_scratch(mats, 4, 1),
        compiler_params=PARAMS,
    )(me, *operands)


def sum_quad(ref):
    return ref[0] + ref[1] + ref[2] + ref[3]


def gather_near_kernel(rows, in_ref, out_ref):
    total = sum_quad(in_ref)
    for place in range(QUAD):
        at = place * FAR
        out_ref[place, : FAR * rows] = total[at * rows : (at + FAR) * rows]
        sums = total[SLOTS * rows + at : SLOTS * rows + at + FAR]
        out_ref[place, FAR * rows : FAR * rows + FAR] = sums
        out_ref[place, FAR * rows + FAR :] = jnp.zeros((8 - FAR, W), jnp.float32)


def gather_near(arrived):
    rows = (arrived.shape[1] - 8) // SLOTS
    return pl.pallas_call(
        functools.partial(gather_near_kernel, rows),
        out_shape=pltpu.VMEM((QUAD, FAR * rows + 8, W), jnp.float32),
        in_specs=[VMEM],
        out_specs=VMEM,
        compiler_params=PARAMS,
    )(pinned(arrived, pltpu.VMEM))


def my_half(me_ref, rows):
    return pl.ds(pl.multiple_of((shifted(me_ref[0], me_ref[1])[0] & 1) * rows, 8), rows)


def gather_far_kernel(me_ref, in_ref, measured_ref, out_ref):
    rows = measured_ref.shape[0]
    total = sum_quad(in_ref)
    out_ref[: FAR * rows] = -total[: FAR * rows]
    out_ref[FAR * rows :] = total[FAR * rows :]
    mine = my_half(me_ref, rows)
    out_ref[mine, :] = out_ref[mine, :] + measured_ref[...]


def gather_far(me, arrived, measured):
    return pl.pallas_call(
        gather_far_kernel,
        out_shape=pltpu.VMEM(arrived.shape[1:], jnp.float32),
        in_specs=[SMEM, VMEM, VMEM],
        out_specs=VMEM,
        compiler_params=PARAMS,
    )(me, pinned(arrived, pltpu.VMEM), pinned(measured, pltpu.VMEM))


def spread_far_kernel(own_ref, came_ref, out_ref):
    rows = out_ref.shape[1] // FAR
    both = own_ref[...] + came_ref[...]
    for half in range(FAR):
        at = FAR * rows + half
        value = both[half * rows : (half + 1) * rows] * (1.0 / both[at : at + 1])
        for place in range(QUAD):
            out_ref[place, half * rows : (half + 1) * rows] = value


def spread_far(own, came):
    rows = (own.shape[0] - 8) // FAR
    return pl.pallas_call(
        spread_far_kernel,
        out_shape=pltpu.VMEM((QUAD, FAR * rows, W), jnp.float32),
        in_specs=[VMEM, VMEM],
        out_specs=VMEM,
        compiler_params=PARAMS,
    )(pinned(own, pltpu.VMEM), pinned(came, pltpu.VMEM))


def spread_near_kernel(
    me_ref, column_ref, far_ref, first_in, last_in, out_hbm, mine_hbm, first_ref, last_ref, sems
):
    mine = far_ref.at[0, my_half(me_ref, mine_hbm.shape[0])]
    copies = fetch_all(
        [(column_ref, out_hbm.at[place]) for place in range(QUAD)] + [(mine, mine_hbm)], sems
    )
    first_ref[...] = first_in[...]
    last_ref[...] = last_in[...]
    for copy in copies:
        copy.wait()


def spread_near(me, column, far, first, last):
    face = jax.ShapeDtypeStruct(first.shape, jnp.float32)
    return pl.pallas_call(
        spread_near_kernel,
        out_shape=[
            pltpu.HBM((QUAD,) + column.shape, jnp.float32),
            pltpu.HBM(column.shape[1:], jnp.float32),
            face,
            face,
        ],
        in_specs=[SMEM] + [VMEM] * 4,
        out_specs=[ANY, ANY, VMEM, VMEM],
        scratch_shapes=[pltpu.SemaphoreType.DMA((QUAD + 1,))],
        compiler_params=PARAMS,
    )(me, *(pinned(a, pltpu.VMEM) for a in (column, far, first, last)))


def back_kernel(
    me_ref, lists_hbm, owners_hbm, starts_hbm, mats_hbm, base_ref, got_ref, out_ref,
    lists, owners, starts, total, mats, sems, mat_sems,
):
    rows, cols = base_ref.shape
    count = mats.shape[0]
    copies = fetch_all([(lists_hbm, lists), (owners_hbm, owners), (starts_hbm, starts)], sems)
    mat_copies = fetch_mats(mats_hbm, mats, mat_sems)
    total[...] = jnp.zeros(total.shape, jnp.float32)
    for copy in copies:
        copy.wait()
    me, core = me_ref[0], me_ref[1]
    for k in range(count):
        start = starts[0, k]
        near, far = near_far(owners[0, lists[k, me]], me, core)
        base = pl.multiple_of(start & -LANES, LANES)
        wait_mats(mat_copies, k, count)
        product = lax.dot_general(
            with_ones(got_ref[near, far]),
            mats[k],
            (((1,), (1,)), ((), ())),
            preferred_element_type=jnp.float32,
        )
        value = jnp.concatenate([join3(product, rows), product[3 * rows : 3 * rows + 8]], axis=0)
        value = jnp.concatenate([value, jnp.zeros((rows + 8, LANES), jnp.float32)], axis=1)
        total[:, pl.ds(base, W + LANES)] += pltpu.roll(value, start & (LANES - 1), 1)
    scale = relax / jnp.maximum(total[rows : rows + 1, :cols], 1.0)
    out_ref[...] = base_ref[...] + total[:rows, :cols] * scale


def back_project(me, lists, owners, starts, base, mats, got):
    rows, cols = base.shape
    operands = [pinned(a, pltpu.HBM) for a in (lists, owners, starts, mats)]
    operands += [pinned(a, pltpu.VMEM) for a in (base, got)]
    return pl.pallas_call(
        back_kernel,
        out_shape=jax.ShapeDtypeStruct((rows, cols), jnp.float32),
        in_specs=[SMEM] + [ANY] * 4 + [VMEM] * 2,
        out_specs=VMEM,
        scratch_shapes=small_scratch(lists, owners, starts)
        + [pltpu.VMEM((rows + 8, cols + LANES), jnp.float32)]
        + mats_scratch(mats, 3, 2),
        compiler_params=PARAMS,
    )(me, *operands)


def with_faces(volume, first, last):
    count = lax.axis_size("gz")
    up = [(i, i + 1) for i in range(count - 1)]
    down = [(i + 1, i) for i in range(count - 1)]
    return jnp.concatenate(
        [lax.ppermute(last, "gz", up), volume, lax.ppermute(first, "gz", down)], axis=0
    )


def total_variation(padded):
    diffs = padded[1:] - padded[:-1]
    slopes = diffs / jnp.sqrt(diffs * diffs + smooth_sq)
    return slopes[:-1] - slopes[1:]


def per_device(volume, sinogram, ray_mats, offsets, ray_lists, owner_map):
    rows = volume.shape[0]
    core = lax.axis_index("gz") % 2
    device = lax.axis_index("xy")
    me = jnp.stack([device, core]).astype(jnp.int32)
    plan = (me, ray_lists.T, owner_map.reshape(1, -1), offsets)
    outgoing, first, last = project(*plan, volume, ray_mats)
    part = gather_far(me, exchange(gather_near(exchange(outgoing, 1)), 2), sinogram)
    far = spread_far(part, swap_far(part))
    column = exchange(far, 2).reshape(SLOTS, rows, W)
    spread, weighted, first, last = spread_near(me, column, far, first, last)
    base = volume - tv_weight * total_variation(with_faces(volume, first, last))
    got = exchange(spread, 1)
    new_volume = back_project(*plan, base, ray_mats, got)
    return (new_volume, weighted)


def solution(mesh):
    in_specs = (P("gz", "xy"), P("gz", "xy"), P("xy", None, None, None), P("xy", None), P(), P())
    out_specs = (P("gz", "xy"), P("gz", "xy"))
    return jax.shard_map(
        per_device, mesh=mesh, in_specs=in_specs, out_specs=out_specs, check_vma=False
    )
```
